512 devices in a mesh: rep: 8 (over x, core), feat: 64 (over z, y).
Axes of the slice: x: 4, y: 4, z: 16, core: 2. Of those that a mesh axis runs over, the one named last changes fastest.
Arguments:
- features: bfloat16 [8, 768, 32768], P('rep', 'feat'), may hold values from -6 to 6
- w_self: bfloat16 [768, 256], P('feat'), may hold values from -0.21875 to 0.21875
- w_neighbor: bfloat16 [768, 256], P('feat'), may hold values from -0.4375 to 0.4375
- tile_list: int32 [192, 16], P('rep'), may hold values from 0 to 255
- nbr_slot: int32 [24576, 10], P('rep'), may hold values from 0 to 2047
- seed_ids: int32 [24576], P('rep'), may hold values from 0 to 32767
- d_hidden: bfloat16 [24576, 256], P(('rep', 'feat')), may hold values from -6 to 6
Outputs:
- hidden: bfloat16 [24576, 256], P(('rep', 'feat'))
- grad_self: float32 [768, 256], P('feat')
- grad_neighbor: float32 [768, 256], P('feat')
The draws below stay inside these ranges and needn't reach their ends.
Inputs may be any that keep to these rules, and one draw needn't show every extreme that they name: `tile_list`: source tile ids of the minibatch. `nbr_slot`: a position in the concatenation of the tile's 16 listed tiles.
All inputs are finite; a program needn't handle non-finite values.
Results may differ from the reference program's by a relative error of at most 0.014.
Values may be sent and summed in bfloat16 or wider, within the bound.
A program may use at most 64 MiB of HBM per device.

```python
import jax
import jax.numpy as jnp

F = 768
H = 256
TILE = 128
FAN = 10
TILES = 16
TB = 24
NS = 256
TARGETS = 3072
SOURCES = 32768
GROUPS = 8
N_REP = 8


def with_ends(array, rng, least, largest):
    spot = [jax.random.randint(jax.random.fold_in(rng, axis), (), 0, length) for axis, length in enumerate(array.shape)]
    longest = array.shape.index(max(array.shape))
    beside = spot[:longest] + [(spot[longest] + 1) % array.shape[longest]] + spot[longest + 1:]
    return array.at[tuple(spot)].set(least).at[tuple(beside)].set(largest)


def level_of(own_key, dims, split, smallest, top_value):
    gain = 1.0
    for dim, parts in split:
        heights = jax.random.uniform(jax.random.fold_in(jax.random.fold_in(own_key, 6), dim), (parts,), jnp.float32, smallest / len(split), top_value / len(split))
        gain = gain * jnp.repeat(jnp.exp(heights), dims[dim] // parts).reshape((-1,) + (1,) * (len(dims) - 1 - dim))
    return gain


def scatter_about(key, extent, deviation, reach, pieces=(), kind=jnp.bfloat16):
    drawn = deviation * jax.random.normal(key, extent, jnp.float32)
    if pieces:
        drawn = drawn * level_of(key, extent, pieces, -0.22, 0.18)
    return jnp.clip(drawn, -reach, reach).astype(kind)


def setup_inputs(seed: int = 0) -> dict:
    key_list = jax.random.split(jax.random.key(seed), 8)
    return {
        "features": scatter_about(key_list[0], (GROUPS, F, SOURCES), 1.0, 6.0, ((0, 8), (1, 64))),
        "w_self": scatter_about(key_list[1], (F, H), F ** -0.5, 0.21875, ((0, 64),)),
        "w_neighbor": scatter_about(key_list[2], (F, H), (F // 4) ** -0.5, 0.4375, ((0, 64),)),
        "tile_list": with_ends(jax.random.randint(key_list[3], (GROUPS * TB, TILES), 0, NS), jax.random.fold_in(key_list[3], 1), 0, NS - 1).astype(jnp.int32),
        "nbr_slot": with_ends(jax.random.randint(key_list[4], (GROUPS * TARGETS, FAN), 0, TILES * TILE), jax.random.fold_in(key_list[4], 1), 0, (TILES * TILE) - 1).astype(jnp.int32),
        "seed_ids": with_ends(jax.random.randint(key_list[5], (GROUPS * TARGETS,), 0, SOURCES), jax.random.fold_in(key_list[5], 1), 0, SOURCES - 1).astype(jnp.int32),
        "d_hidden": scatter_about(key_list[6], (GROUPS * TARGETS, H), 1.0, 6.0, ((0, 512),)),
    }


def reference(features, w_self, w_neighbor, tile_list, nbr_slot, seed_ids, d_hidden):
    outputs = []
    grad_self = jnp.zeros((F, H), jnp.float32)
    grad_neighbor = jnp.zeros((F, H), jnp.float32)
    self_weight = w_self.astype(jnp.float32)
    mean_weight = w_neighbor.astype(jnp.float32)
    for group in range(N_REP):
        local_feat = features[group]
        seeds = seed_ids[group * TARGETS:(group + 1) * TARGETS]
        self_feat = jnp.take(local_feat, seeds, axis=1)
        tiles = tile_list[group * TB:(group + 1) * TB]
        slots = nbr_slot[group * TARGETS:(group + 1) * TARGETS]
        owner_tile = (jnp.arange(TARGETS, dtype=jnp.int32) // TILE).astype(jnp.int32)
        chosen = tiles[owner_tile[:, None], slots // TILE]
        source_ids = (chosen * TILE + slots % TILE).astype(jnp.int32)
        picked = jnp.take(local_feat, source_ids, axis=1).astype(jnp.float32)
        neighbor_mean = (jnp.sum(picked, axis=2) * (1.0 / FAN)).astype(jnp.bfloat16)
        own_wide = self_feat.astype(jnp.float32)
        mean_wide = neighbor_mean.astype(jnp.float32)
        pre = jnp.dot(own_wide.T, self_weight) + jnp.dot(mean_wide.T, mean_weight)
        outputs.append(jax.nn.silu(pre).astype(jnp.bfloat16))
        sigma = jax.nn.sigmoid(pre)
        cotangent = d_hidden[group * TARGETS:(group + 1) * TARGETS].astype(jnp.float32)
        d_pre = (cotangent * sigma * (1.0 + pre * (1.0 - sigma))).astype(jnp.bfloat16)
        d_wide = d_pre.astype(jnp.float32)
        grad_self = grad_self + jnp.dot(own_wide, d_wide)
        grad_neighbor = grad_neighbor + jnp.dot(mean_wide, d_wide)
    return jnp.concatenate(outputs, axis=0), grad_self, grad_neighbor
```

```python
import jax
import jax.numpy as jnp
from jax import lax
from jax.experimental import pallas as pl
from jax.experimental.pallas import tpu as pltpu
from jax.sharding import PartitionSpec as P

MESH = pl.DeviceIdType.MESH
F32, BF16 = jnp.float32, jnp.bfloat16
NZ, NY, NR = 16, 4, 8
TILE, TB, FAN, LISTED, NS = 128, 24, 10, 16, 256
WIDTH = 12
ROWS = 2 * WIDTH
OWN = 48
H = 256


def lane_pick(values, lanes):
    return jnp.take_along_axis(values, lanes, axis=1, mode="promise_in_bounds")


def select_tree(level, bits):
    for bit in bits:
        level = [jnp.where(bit, level[i + 1], level[i]) for i in range(0, len(level), 2)]
    return level[0]


def neighbor_sums(tiles_ref, x_ref, slot_ref, t):
    low, high = [], []
    for k in range(LISTED):
        at = pl.multiple_of(tiles_ref[t, k] * TILE, TILE)
        block = x_ref[:, pl.ds(at, TILE)].astype(F32)
        low.append(block[:8])
        high.append(block[8:])
    pairs = [jnp.concatenate(high[k:k + 2], axis=0) for k in range(0, LISTED, 2)]
    upper = lax.broadcasted_iota(jnp.int32, (8, TILE), 0) >= 4
    total_low = jnp.zeros((8, TILE), F32)
    total_pair = jnp.zeros((8, TILE), F32)
    for j in range(FAN):
        slot = jnp.broadcast_to(slot_ref[t, j:j + 1, :], (8, TILE))
        lane = slot & (TILE - 1)
        bits = [(slot & (TILE << b)) != 0 for b in range(4)]
        total_low += select_tree([lane_pick(v, lane) for v in low], bits)
        picked = select_tree([lane_pick(v, lane) for v in pairs], bits[1:])
        total_pair += jnp.where(bits[0] == upper, picked, 0.0)
    return total_low, total_pair[:4] + total_pair[4:]


def gather_kernel(tiles_ref, x_ref, slot_ref, seed_ref, g_ref, wide, turned, rows):
    def fill(k, _):
        block = x_ref[:, pl.ds(pl.multiple_of(k * TILE, TILE), TILE)]
        wide[pl.ds(pl.multiple_of(k * 16, 16), WIDTH)] = block.astype(F32)
        return 0

    lax.fori_loop(0, NS, fill, 0, unroll=8)
    for f in range(WIDTH):
        turned[f] = wide[pl.ds(f, NS, stride=16)].T.astype(BF16)

    def three_tiles(u, _):
        span = 3 * TILE
        seed = jnp.concatenate([seed_ref[3 * u + i] for i in range(3)], axis=1)
        hot = (lax.broadcasted_iota(jnp.int32, (NS, span), 0) == (seed >> 7)).astype(F32).astype(BF16)
        mask = lax.broadcasted_iota(jnp.int32, (TILE, span), 0) == (seed & (TILE - 1))
        for f in range(WIDTH):
            columns = jnp.dot(turned[f], hot, preferred_element_type=F32)
            row = jnp.sum(jnp.where(mask, columns, 0.0), axis=0, keepdims=True)
            for i in range(3):
                rows[i, f:f + 1] = row[:, i * TILE:(i + 1) * TILE]
        for i in range(3):
            low, high = neighbor_sums(tiles_ref, x_ref, slot_ref, 3 * u + i)
            rows[i, WIDTH:16] = high * (1.0 / FAN)
            rows[i, 16:ROWS] = low * (1.0 / FAN)
        first, middle, last = rows[0], rows[1], rows[2]
        front = lax.broadcasted_iota(jnp.int32, (ROWS, TILE), 1) < TILE // 2
        middle_turned = pltpu.roll(middle, TILE // 2, 1)
        last_turned = pltpu.roll(last, TILE // 2, 1)
        g_ref[2 * u] = jnp.concatenate([first, jnp.where(front, middle, 0.0)], axis=0).astype(BF16)
        g_ref[2 * u + 1] = jnp.concatenate(
            [jnp.where(front, middle_turned, last_turned), jnp.where(front, last_turned, 0.0)], axis=0
        ).astype(BF16)
        return 0

    lax.fori_loop(0, TB // 3, three_tiles, 0)


def gather(features, tile_list, nbr_slot, seed_ids):
    slots = jnp.transpose(nbr_slot.reshape(TB, TILE, FAN), (0, 2, 1))
    vmem = pl.BlockSpec(memory_space=pltpu.VMEM)
    return pl.pallas_call(
        gather_kernel,
        out_shape=jax.ShapeDtypeStruct((NZ, 2 * ROWS, TILE), BF16),
        in_specs=[pl.BlockSpec(memory_space=pltpu.SMEM), vmem, vmem, vmem],
        out_specs=vmem,
        scratch_shapes=[
            pltpu.VMEM((NS * 16, TILE), F32),
            pltpu.VMEM((WIDTH, TILE, NS), BF16),
            pltpu.VMEM((3, ROWS, TILE), F32),
        ],
        compiler_params=pltpu.CompilerParams(vmem_limit_bytes=32 * 2**20),
        name="gather",
    )(tile_list, features, slots, seed_ids.reshape(TB, 1, TILE))


def exchange_kernel(
    g_ref, ws_ref, wn_ref, dh_ref, hid_ref, gs_ref, gn_ref,
    xb, wb, pf, ps, pr, db, qf, qs, qr, es, er,
    x_out, x_in, w_out, w_in, p_out, p_in, d_out, d_in, q_out, q_in, e_out, e_in,
):
    rep = lax.axis_index("rep")
    feat = lax.axis_index("feat")
    z, y = feat // NY, feat % NY

    def along_z(o):
        return rep, lax.rem(z + o, NZ) * NY + y

    def along_y(o):
        return rep, z * NY + lax.rem(y + o, NY)

    def along_rep(o):
        return lax.rem(rep + o, NR), feat

    barrier = pltpu.get_barrier_semaphore()

    def greet(way):
        def step(o, _):
            pl.semaphore_signal(barrier, inc=1, device_id=way(o), device_id_type=MESH)
            return 0
        return step

    lax.fori_loop(1, NZ, greet(along_z), 0)
    lax.fori_loop(1, NY, greet(along_y), 0)
    lax.fori_loop(1, NR, greet(along_rep), 0)

    mean_weight = wn_ref[...].astype(F32)
    wb[z] = jnp.concatenate(
        [ws_ref[...].astype(F32), mean_weight[8:], mean_weight[:8], jnp.zeros((8, H), F32)], axis=0
    ).astype(BF16)
    xb[z] = g_ref[z]

    pl.semaphore_wait(barrier, NZ + NY + NR - 3)

    def copy(src, dst, out_sem, in_sem, o, target):
        return pltpu.make_async_remote_copy(
            src_ref=src, dst_ref=dst, send_sem=out_sem.at[o], recv_sem=in_sem.at[o],
            device_id=target, device_id_type=MESH,
        )

    def each(count, body):
        def step(o, _):
            body(o)
            return 0
        lax.fori_loop(1, count, step, 0)

    def x_copy(o, slot):
        return copy(g_ref.at[lax.rem(z + o, NZ)], xb.at[slot], x_out, x_in, o, along_z(o))

    def w_copy(o, slot):
        return copy(wb.at[z], wb.at[slot], w_out, w_in, o, along_z(o))

    def p_copy(o, slot):
        return copy(ps.at[lax.rem(y + o, NY)], pr.at[slot], p_out, p_in, o, along_y(o))

    def d_copy(o, slot):
        return copy(db.at[y], db.at[slot], d_out, d_in, o, along_y(o))

    def q_copy(o, slot):
        return copy(qs.at[lax.rem(z + o, NZ)], qr.at[slot], q_out, q_in, o, along_z(o))

    def e_copy(o, slot):
        return copy(es, er.at[slot], e_out, e_in, o, along_rep(o))

    def behind(place, o, count):
        return lax.rem(place + count - o, count)

    each(NZ, lambda o: x_copy(o, z).start())
    each(NZ, lambda o: w_copy(o, z).start())
    each(NZ, lambda o: w_copy(o, behind(z, o, NZ)).wait_recv())
    each(NZ, lambda o: x_copy(o, behind(z, o, NZ)).wait_recv())

    wide = xb[...].astype(F32)
    x = jnp.concatenate([wide[:, :ROWS], wide[:, ROWS:]], axis=2).reshape(NZ * ROWS, 2 * TILE).astype(BF16)
    w = wb[...].astype(F32)[:, :ROWS].reshape(NZ * ROWS, H).astype(BF16)
    part = lax.dot_general(x, w, (((0,), (0,)), ((), ())), preferred_element_type=F32)
    for i in range(NY):
        pf[i] = part[i * OWN:(i + 1) * OWN]
        ps[i] = part[i * OWN:(i + 1) * OWN].astype(BF16)
    each(NY, lambda o: p_copy(o, y).start())
    pr[y] = jnp.zeros((OWN, H), BF16)
    each(NY, lambda o: p_copy(o, behind(y, o, NY)).wait_recv())
    pre = pf[y] + jnp.sum(pr[...].astype(F32), axis=0)

    sigma = jax.nn.sigmoid(pre)
    db[y] = (dh_ref[...].astype(F32) * sigma * (1.0 + pre * (1.0 - sigma))).astype(BF16)
    each(NY, lambda o: d_copy(o, y).start())
    hid_ref[...] = (pre * sigma).astype(BF16)
    each(NY, lambda o: d_copy(o, behind(y, o, NY)).wait_recv())

    d_pre = jnp.concatenate(
        [db[...].reshape(NY * OWN, H), jnp.zeros((2 * TILE - NY * OWN, H), BF16)], axis=0
    )
    grad = jnp.dot(x, d_pre, preferred_element_type=F32).reshape(NZ, ROWS, H)
    grad = jnp.concatenate([grad[:, :, :TILE], grad[:, :, TILE:]], axis=1)
    qf[...] = grad
    qs[...] = grad.astype(BF16)
    each(NZ, lambda o: q_copy(o, z).start())
    qr[z] = jnp.zeros((2 * ROWS, TILE), BF16)
    each(NZ, lambda o: q_copy(o, behind(z, o, NZ)).wait_recv())
    mine = qf[z] + jnp.sum(qr[...].astype(F32), axis=0)

    es[...] = mine.astype(BF16)
    each(NR, lambda o: e_copy(o, rep).start())
    er[rep] = mine.astype(BF16)
    each(NR, lambda o: e_copy(o, behind(rep, o, NR)).wait_recv())
    total = jnp.sum(er[...].astype(F32), axis=0)
    total = jnp.concatenate([total[:ROWS], total[ROWS:]], axis=1)
    gs_ref[...] = total[:WIDTH]
    gn_ref[:8] = total[16:]
    gn_ref[8:] = total[WIDTH:16]

    each(NZ, lambda o: x_copy(o, z).wait_send())
    each(NZ, lambda o: w_copy(o, z).wait_send())
    each(NY, lambda o: p_copy(o, y).wait_send())
    each(NY, lambda o: d_copy(o, y).wait_send())
    each(NZ, lambda o: q_copy(o, z).wait_send())
    each(NR, lambda o: e_copy(o, rep).wait_send())


def exchange(gathered, w_self, w_neighbor, d_hidden):
    vmem = pl.BlockSpec(memory_space=pltpu.VMEM)
    dma = pltpu.SemaphoreType.DMA
    return pl.pallas_call(
        exchange_kernel,
        out_shape=(
            jax.ShapeDtypeStruct((OWN, H), BF16),
            jax.ShapeDtypeStruct((WIDTH, H), F32),
            jax.ShapeDtypeStruct((WIDTH, H), F32),
        ),
        in_specs=[vmem] * 4,
        out_specs=(vmem,) * 3,
        scratch_shapes=[
            pltpu.VMEM((NZ, 2 * ROWS, TILE), BF16),
            pltpu.VMEM((NZ, 32, H), BF16),
            pltpu.VMEM((NY, OWN, H), F32),
            pltpu.VMEM((NY, OWN, H), BF16),
            pltpu.VMEM((NY, OWN, H), BF16),
            pltpu.VMEM((NY, OWN, H), BF16),
            pltpu.VMEM((NZ, 2 * ROWS, TILE), F32),
            pltpu.VMEM((NZ, 2 * ROWS, TILE), BF16),
            pltpu.VMEM((NZ, 2 * ROWS, TILE), BF16),
            pltpu.VMEM((2 * ROWS, TILE), BF16),
            pltpu.VMEM((NR, 2 * ROWS, TILE), BF16),
        ]
        + [dma((n,)) for n in (NZ, NZ, NZ, NZ, NY, NY, NY, NY, NZ, NZ, NR, NR)],
        compiler_params=pltpu.CompilerParams(
            collective_id=0, has_side_effects=True, vmem_limit_bytes=32 * 2**20
        ),
        name="exchange",
    )(gathered, w_self, w_neighbor, d_hidden)


def local(features, w_self, w_neighbor, tile_list, nbr_slot, seed_ids, d_hidden):
    gathered = gather(features[0], tile_list, nbr_slot, seed_ids)
    return exchange(gathered, w_self, w_neighbor, d_hidden)


def solution(mesh):
    placed = (
        P("rep", "feat", None),
        P("feat", None),
        P("feat", None),
        P("rep", None),
        P("rep", None),
        P("rep"),
        P(("rep", "feat"), None),
    )
    return jax.shard_map(
        local,
        mesh=mesh,
        in_specs=placed,
        out_specs=(P(("rep", "feat"), None), P("feat", None), P("feat", None)),
        check_vma=False,
    )
```

```python
import jax
import jax.numpy as jnp
from jax import lax
from jax.experimental import pallas as pl
from jax.experimental.pallas import tpu as pltpu
from jax.sharding import PartitionSpec as P

MESH = pl.DeviceIdType.MESH
F32, BF16 = jnp.float32, jnp.bfloat16
NZ, NY, NR = 16, 4, 8
TILE, TB, FAN, LISTED, NS = 128, 24, 10, 16, 256
WIDTH = 12
ROWS = 2 * WIDTH
OWN = 48
H = 256
CHUNKS = 4
SPREAD = 4


def lane_pick(values, lanes):
    return jnp.take_along_axis(values, lanes, axis=1, mode="promise_in_bounds")


def select_tree(level, bits):
    for bit in bits:
        level = [jnp.where(bit, level[i + 1], level[i]) for i in range(0, len(level), 2)]
    return level[0]


def neighbor_sums(tiles_ref, wide, slot_ref, t):
    low, high = [], []
    for k in range(LISTED):
        block = wide[tiles_ref[k, t]]
        low.append(block[:8])
        high.append(block[8:WIDTH])
    pairs = [jnp.concatenate(high[k:k + 2], axis=0) for k in range(0, LISTED, 2)]
    upper = lax.broadcasted_iota(jnp.int32, (8, TILE), 0) >= 4
    total_low = jnp.zeros((8, TILE), F32)
    total_pair = jnp.zeros((8, TILE), F32)
    targets = pl.ds(pl.multiple_of(t * TILE, TILE), TILE)
    for j in range(FAN):
        slot = jnp.broadcast_to(slot_ref[j:j + 1, targets], (8, TILE))
        lane = slot & (TILE - 1)
        bits = [(slot & (TILE << b)) != 0 for b in range(4)]
        total_low += select_tree([lane_pick(v, lane) for v in low], bits)
        picked = select_tree([lane_pick(v, lane) for v in pairs], bits[1:])
        total_pair += jnp.where(bits[0] == upper, picked, 0.0)
    return total_low, total_pair[:4] + total_pair[4:]


def prepare(x_ref, wide, first_tile, tiles):
    def fill(k, _):
        block = x_ref[:, pl.ds(pl.multiple_of(k * TILE, TILE), TILE)]
        wide[k, :WIDTH] = block.astype(F32)
        return 0

    lax.fori_loop(first_tile, first_tile + tiles, fill, 0, unroll=8)


def gather_blocks(tiles_ref, wide, slot_ref, seed_ref, turned, rows, gb, u):
    span = 3 * TILE
    seed = jnp.concatenate([seed_ref[3 * u + i] for i in range(3)], axis=1)
    hot = (lax.broadcasted_iota(jnp.int32, (NS, span), 0) == (seed >> 7)).astype(F32).astype(BF16)
    mask = lax.broadcasted_iota(jnp.int32, (TILE, span), 0) == (seed & (TILE - 1))
    for f in range(WIDTH):
        columns = jnp.dot(turned[f], hot, preferred_element_type=F32)
        row = jnp.sum(jnp.where(mask, columns, 0.0), axis=0, keepdims=True)
        for i in range(3):
            rows[i, f:f + 1] = row[:, i * TILE:(i + 1) * TILE]
    for i in range(3):
        low, high = neighbor_sums(tiles_ref, wide, slot_ref, 3 * u + i)
        rows[i, WIDTH:16] = high * (1.0 / FAN)
        rows[i, 16:ROWS] = low * (1.0 / FAN)
    first, middle, last = rows[0], rows[1], rows[2]
    front = lax.broadcasted_iota(jnp.int32, (ROWS, TILE), 1) < TILE // 2
    middle_turned = pltpu.roll(middle, TILE // 2, 1)
    last_turned = pltpu.roll(last, TILE // 2, 1)
    gb[2 * u] = jnp.concatenate([first, jnp.where(front, middle, 0.0)], axis=0).astype(BF16)
    gb[2 * u + 1] = jnp.concatenate(
        [jnp.where(front, middle_turned, last_turned), jnp.where(front, last_turned, 0.0)], axis=0
    ).astype(BF16)


def sage_kernel(
    x_hbm, tiles_hbm, slot_hbm, seed_hbm, ws_ref, wn_ref, dh_ref, hid_ref, gs_ref, gn_ref,
    x_ref, tiles_ref, slot_ref, seed_ref, wide, turned, rows, gb,
    xb, wb, pf, ps, pr, db, qf, qs, qr, es, er,
    l_in, x_out, x_in, w_out, w_in, v_out, v_in, p_out, p_in, d_out, d_in, q_out, q_in, e_out, e_in,
):
    rep = lax.axis_index("rep")
    feat = lax.axis_index("feat")
    z, y = feat // NY, feat % NY
    chunk = NS * TILE // CHUNKS

    loads = [
        pltpu.make_async_copy(
            x_hbm.at[:, pl.ds(i * chunk, chunk)], x_ref.at[:, pl.ds(i * chunk, chunk)], l_in.at[i]
        )
        for i in range(CHUNKS)
    ] + [
        pltpu.make_async_copy(tiles_hbm, tiles_ref, l_in.at[CHUNKS]),
        pltpu.make_async_copy(slot_hbm, slot_ref, l_in.at[CHUNKS + 1]),
        pltpu.make_async_copy(seed_hbm, seed_ref, l_in.at[CHUNKS + 2]),
    ]
    for load in loads:
        load.start()

    def along_z(o):
        return rep, lax.rem(z + o, NZ) * NY + y

    def along_y(o):
        return rep, z * NY + lax.rem(y + o, NY)

    def along_rep(o):
        return lax.rem(rep + o, NR), feat

    barrier = pltpu.get_barrier_semaphore()

    def each(count, body):
        def step(o, _):
            body(o)
            return 0
        lax.fori_loop(1, count, step, 0)

    def greet(way):
        return lambda o: pl.semaphore_signal(barrier, inc=1, device_id=way(o), device_id_type=MESH)

    each(NZ, greet(along_z))
    each(NY, greet(along_y))
    each(NR, greet(along_rep))

    def copy(src, dst, out_sem, in_sem, o, target):
        return pltpu.make_async_remote_copy(
            src_ref=src, dst_ref=dst, send_sem=out_sem.at[o], recv_sem=in_sem.at[o],
            device_id=target, device_id_type=MESH,
        )

    def x_copy(o, slot):
        return copy(gb.at[lax.rem(z + o, NZ)], xb.at[slot], x_out, x_in, o, along_z(o))

    def w_copy(o, slot):
        return copy(wb.at[z], wb.at[slot], w_out, w_in, o, along_z(o))

    def v_copy(half, o, slot):
        return pltpu.make_async_remote_copy(
            src_ref=wb.at[slot], dst_ref=wb.at[slot], send_sem=v_out.at[half, o], recv_sem=v_in.at[half, o],
            device_id=along_rep(o), device_id_type=MESH,
        )

    def p_copy(o, slot):
        return copy(ps.at[lax.rem(y + o, NY)], pr.at[slot], p_out, p_in, o, along_y(o))

    def d_copy(o, slot):
        return copy(db.at[y], db.at[slot], d_out, d_in, o, along_y(o))

    def q_copy(o, slot):
        return copy(qs.at[lax.rem(z + o, NZ)], qr.at[slot], q_out, q_in, o, along_z(o))

    def e_copy(o, slot):
        return copy(es, er.at[slot], e_out, e_in, o, along_rep(o))

    def behind(place, o, count):
        return lax.rem(place + count - o, count)

    pl.semaphore_wait(barrier, NZ + NY + NR - 3)

    @pl.when(lax.rem(z, NR) == rep)
    def _():
        mean_weight = wn_ref[...].astype(F32)
        weights = jnp.concatenate([ws_ref[...].astype(F32), mean_weight[8:], mean_weight[:8]], axis=0)
        wb[z] = jnp.concatenate([weights[:, :TILE], weights[:, TILE:]], axis=0).astype(BF16)
        each(NZ, lambda o: w_copy(o, z).start())

    for i in range(CHUNKS):
        loads[i].wait()
        prepare(x_ref, wide, i * (NS // CHUNKS), NS // CHUNKS)
    for f in range(WIDTH):
        turned[f] = wide[:, f].T.astype(BF16)
    for load in loads[CHUNKS:]:
        load.wait()

    def two_blocks(i, _):
        odd = i % 2
        away = odd * (4 - (i + 1) // 2) + (1 - odd) * (4 + i // 2)
        u = (z // 2 + away) % (NZ // 2)
        gather_blocks(tiles_ref, wide, slot_ref, seed_ref, turned, rows, gb, u)
        for e in range(2):
            o = (2 * u + e + NZ - z) % NZ

            @pl.when(o != 0)
            def _():
                x_copy(o, z).start()

            @pl.when(o == 0)
            def _():
                xb[z] = gb[z]

        @pl.when(i == SPREAD)
        def _():
            for half in range(2):
                source = rep + half * NR

                @pl.when(source != z)
                def _():
                    w_copy((z + NZ - source) % NZ, source).wait_recv()

                each(NR, lambda o: v_copy(half, o, source).start())

        return 0

    lax.fori_loop(0, NZ // 2, two_blocks, 0)

    for half in range(2):
        each(NR, lambda o: v_copy(half, o, behind(rep, o, NR) + half * NR).wait_recv())
    w = wb[...].astype(F32)
    w = jnp.concatenate([w[:, :ROWS], w[:, ROWS:]], axis=2).reshape(NZ * ROWS, H).astype(BF16)
    each(NZ, lambda o: x_copy(o, behind(z, o, NZ)).wait_recv())
    x = xb[...].astype(F32)
    x = jnp.concatenate([x[:, :ROWS], x[:, ROWS:]], axis=2).reshape(NZ * ROWS, 2 * TILE).astype(BF16)
    part = lax.dot_general(x, w, (((0,), (0,)), ((), ())), preferred_element_type=F32)
    for i in range(NY):
        pf[i] = part[i * OWN:(i + 1) * OWN]
        ps[i] = part[i * OWN:(i + 1) * OWN].astype(BF16)
    each(NY, lambda o: p_copy(o, y).start())
    pr[y] = jnp.zeros((OWN, H), BF16)
    each(NY, lambda o: p_copy(o, behind(y, o, NY)).wait_recv())
    pre = pf[y] + jnp.sum(pr[...].astype(F32), axis=0)

    sigma = jax.nn.sigmoid(pre)
    db[y] = (dh_ref[...].astype(F32) * sigma * (1.0 + pre * (1.0 - sigma))).astype(BF16)
    each(NY, lambda o: d_copy(o, y).start())
    hid_ref[...] = (pre * sigma).astype(BF16)
    each(NY, lambda o: d_copy(o, behind(y, o, NY)).wait_recv())

    d_pre = jnp.concatenate(
        [db[...].reshape(NY * OWN, H), jnp.zeros((2 * TILE - NY * OWN, H), BF16)], axis=0
    )
    grad = jnp.dot(x, d_pre, preferred_element_type=F32).reshape(NZ, ROWS, H)
    grad = jnp.concatenate([grad[:, :, :TILE], grad[:, :, TILE:]], axis=1)
    qf[...] = grad
    qs[...] = grad.astype(BF16)
    each(NZ, lambda o: q_copy(o, z).start())
    qr[z] = jnp.zeros((2 * ROWS, TILE), BF16)
    each(NZ, lambda o: q_copy(o, behind(z, o, NZ)).wait_recv())
    mine = qf[z] + jnp.sum(qr[...].astype(F32), axis=0)

    es[...] = mine.astype(BF16)
    each(NR, lambda o: e_copy(o, rep).start())
    er[rep] = mine.astype(BF16)
    each(NR, lambda o: e_copy(o, behind(rep, o, NR)).wait_recv())
    total = jnp.sum(er[...].astype(F32), axis=0)
    total = jnp.concatenate([total[:ROWS], total[ROWS:]], axis=1)
    gs_ref[...] = total[:WIDTH]
    gn_ref[:8] = total[16:]
    gn_ref[8:] = total[WIDTH:16]

    @pl.when(lax.rem(z, NR) == rep)
    def _():
        each(NZ, lambda o: w_copy(o, z).wait_send())

    for half in range(2):
        each(NR, lambda o: v_copy(half, o, rep + half * NR).wait_send())
    each(NZ, lambda o: x_copy(o, z).wait_send())
    each(NY, lambda o: p_copy(o, y).wait_send())
    each(NY, lambda o: d_copy(o, y).wait_send())
    each(NZ, lambda o: q_copy(o, z).wait_send())
    each(NR, lambda o: e_copy(o, rep).wait_send())


def local(features, w_self, w_neighbor, tile_list, nbr_slot, seed_ids, d_hidden):
    vmem = pl.BlockSpec(memory_space=pltpu.VMEM)
    anywhere = pl.BlockSpec(memory_space=pl.ANY)
    dma = pltpu.SemaphoreType.DMA
    return pl.pallas_call(
        sage_kernel,
        out_shape=(
            jax.ShapeDtypeStruct((OWN, H), BF16),
            jax.ShapeDtypeStruct((WIDTH, H), F32),
            jax.ShapeDtypeStruct((WIDTH, H), F32),
        ),
        in_specs=[anywhere] * 4 + [vmem] * 3,
        out_specs=(vmem,) * 3,
        scratch_shapes=[
            pltpu.VMEM((WIDTH, NS * TILE), BF16),
            pltpu.SMEM((LISTED, TB), jnp.int32),
            pltpu.VMEM((FAN, TB * TILE), jnp.int32),
            pltpu.VMEM((TB, 1, TILE), jnp.int32),
            pltpu.VMEM((NS, 16, TILE), F32),
            pltpu.VMEM((WIDTH, TILE, NS), BF16),
            pltpu.VMEM((3, ROWS, TILE), F32),
            pltpu.VMEM((NZ, 2 * ROWS, TILE), BF16),
            pltpu.VMEM((NZ, 2 * ROWS, TILE), BF16),
            pltpu.VMEM((NZ, 2 * ROWS, TILE), BF16),
            pltpu.VMEM((NY, OWN, H), F32),
            pltpu.VMEM((NY, OWN, H), BF16),
            pltpu.VMEM((NY, OWN, H), BF16),
            pltpu.VMEM((NY, OWN, H), BF16),
            pltpu.VMEM((NZ, 2 * ROWS, TILE), F32),
            pltpu.VMEM((NZ, 2 * ROWS, TILE), BF16),
            pltpu.VMEM((NZ, 2 * ROWS, TILE), BF16),
            pltpu.VMEM((2 * ROWS, TILE), BF16),
            pltpu.VMEM((NR, 2 * ROWS, TILE), BF16),
        ]
        + [dma((CHUNKS + 3,))]
        + [dma((n,)) for n in (NZ, NZ, NZ, NZ)]
        + [dma((2, NR)), dma((2, NR))]
        + [dma((n,)) for n in (NY, NY, NY, NY, NZ, NZ, NR, NR)],
        compiler_params=pltpu.CompilerParams(
            collective_id=0, has_side_effects=True, vmem_limit_bytes=48 * 2**20
        ),
        name="exchange",
    )(
        features[0], tile_list.T, nbr_slot.T, seed_ids.reshape(TB, 1, TILE), w_self, w_neighbor, d_hidden
    )


def solution(mesh):
    placed = (
        P("rep", "feat", None),
        P("feat", None),
        P("feat", None),
        P("rep", None),
        P("rep", None),
        P("rep"),
        P(("rep", "feat"), None),
    )
    return jax.shard_map(
        local,
        mesh=mesh,
        in_specs=placed,
        out_specs=(P(("rep", "feat"), None), P("feat", None), P("feat", None)),
        check_vma=False,
    )
```

```python
import jax
import jax.numpy as jnp
from jax import lax
from jax.experimental import pallas as pl
from jax.experimental.pallas import tpu as pltpu
from jax.sharding import PartitionSpec as P

MESH = pl.DeviceIdType.MESH
F32, BF16 = jnp.float32, jnp.bfloat16
N = 8
TILE, TB, FAN, LISTED, NS = 128, 24, 10, 16, 256
WIDTH = 12
ROWS = 2 * WIDTH
BLOCK = 80
OWN = 48
H = 256
CHUNKS = 4
SPREAD = 4


def lane_pick(values, lanes):
    return jnp.take_along_axis(values, lanes, axis=1, mode="promise_in_bounds")


def select_tree(level, bits):
    for bit in bits:
        level = [jnp.where(bit, level[i + 1], level[i]) for i in range(0, len(level), 2)]
    return level[0]


def neighbor_sums(tiles_ref, wide, slot_ref, t):
    low, high = [], []
    for k in range(LISTED):
        block = wide[tiles_ref[k, t]]
        low.append(block[:8])
        high.append(block[8:WIDTH])
    pairs = [jnp.concatenate(high[k:k + 2], axis=0) for k in range(0, LISTED, 2)]
    upper = lax.broadcasted_iota(jnp.int32, (8, TILE), 0) >= 4
    total_low = jnp.zeros((8, TILE), F32)
    total_pair = jnp.zeros((8, TILE), F32)
    targets = pl.ds(pl.multiple_of(t * TILE, TILE), TILE)
    for j in range(FAN):
        slot = jnp.broadcast_to(slot_ref[j:j + 1, targets], (8, TILE))
        lane = slot & (TILE - 1)
        bits = [(slot & (TILE << b)) != 0 for b in range(4)]
        total_low += select_tree([lane_pick(v, lane) for v in low], bits)
        picked = select_tree([lane_pick(v, lane) for v in pairs], bits[1:])
        total_pair += jnp.where(bits[0] == upper, picked, 0.0)
    return total_low, total_pair[:4] + total_pair[4:]


def gather_block(tiles_ref, wide, slot_ref, seed_ref, turned, rows, u):
    span = 3 * TILE
    seed = jnp.concatenate([seed_ref[3 * u + i] for i in range(3)], axis=1)
    hot = (lax.broadcasted_iota(jnp.int32, (NS, span), 0) == (seed >> 7)).astype(F32).astype(BF16)
    mask = lax.broadcasted_iota(jnp.int32, (TILE, span), 0) == (seed & (TILE - 1))
    for f in range(WIDTH):
        columns = jnp.dot(turned[f], hot, preferred_element_type=F32)
        row = jnp.sum(jnp.where(mask, columns, 0.0), axis=0, keepdims=True)
        for i in range(3):
            rows[ROWS * i + f:ROWS * i + f + 1] = row[:, i * TILE:(i + 1) * TILE]
    for i in range(3):
        low, high = neighbor_sums(tiles_ref, wide, slot_ref, 3 * u + i)
        rows[ROWS * i + WIDTH:ROWS * i + 16] = high * (1.0 / FAN)
        rows[ROWS * i + 16:ROWS * (i + 1)] = low * (1.0 / FAN)
    return jnp.concatenate([rows[...], jnp.zeros((BLOCK - 3 * ROWS, TILE), F32)], axis=0).astype(BF16)


def sage_kernel(
    x_hbm, tiles_hbm, slot_hbm, seed_hbm, ws_hbm, wn_hbm, dh_hbm, hid_ref, gs_ref, gn_ref,
    x_ref, tiles_ref, slot_ref, seed_ref, ws_ref, wn_ref, dh_ref, wide, turned, rows, gb,
    xb, wb, pf, ps, pr, db, qf, qs, qr, es, er,
    l_in, x_out, x_in, w_out, w_in, v_out, v_in, p_out, p_in, d_out, d_in, q_out, q_in, e_out, e_in,
):
    rep = lax.axis_index("rep")
    feat = lax.axis_index("feat")
    b, a = feat // N, feat % N
    chunk = NS * TILE // CHUNKS

    pairs = [
        (x_hbm.at[:, pl.ds(i * chunk, chunk)], x_ref.at[:, pl.ds(i * chunk, chunk)]) for i in range(CHUNKS)
    ] + [
        (tiles_hbm, tiles_ref), (slot_hbm, slot_ref), (seed_hbm, seed_ref),
        (ws_hbm, ws_ref), (wn_hbm, wn_ref), (dh_hbm, dh_ref),
    ]
    loads = [pltpu.make_async_copy(src, dst, l_in.at[i]) for i, (src, dst) in enumerate(pairs)]
    for load in loads:
        load.start()

    def ahead(place, o):
        return lax.rem(place + o, N)

    def behind(place, o):
        return lax.rem(place + N - o, N)

    def along_b(o):
        return rep, ahead(b, o) * N + a

    def along_a(o):
        return rep, b * N + ahead(a, o)

    def along_rep(o):
        return ahead(rep, o), feat

    barrier = pltpu.get_barrier_semaphore()

    def each(body):
        def step(o, _):
            body(o)
            return 0
        lax.fori_loop(1, N, step, 0)

    def greet(way):
        return lambda o: pl.semaphore_signal(barrier, inc=1, device_id=way(o), device_id_type=MESH)

    each(greet(along_b))
    each(greet(along_a))
    each(greet(along_rep))

    def copy(src, dst, out_sem, in_sem, o, target):
        return pltpu.make_async_remote_copy(
            src_ref=src, dst_ref=dst, send_sem=out_sem.at[o], recv_sem=in_sem.at[o],
            device_id=target, device_id_type=MESH,
        )

    def x_copy(o, slot):
        return copy(gb.at[ahead(b, o)], xb.at[slot], x_out, x_in, o, along_b(o))

    def w_copy(o, slot):
        return copy(wb.at[b], wb.at[slot], w_out, w_in, o, along_b(o))

    def v_copy(o, slot):
        return copy(wb.at[rep], wb.at[slot], v_out, v_in, o, along_rep(o))

    def p_copy(o, slot):
        return copy(ps.at[ahead(a, o)], pr.at[slot], p_out, p_in, o, along_a(o))

    def d_copy(o, slot):
        return copy(db.at[a], db.at[slot], d_out, d_in, o, along_a(o))

    def q_copy(o, slot):
        return copy(qs.at[ahead(b, o)], qr.at[slot], q_out, q_in, o, along_b(o))

    def e_copy(o, slot):
        return copy(es, er.at[slot], e_out, e_in, o, along_rep(o))

    def fill(k, _):
        wide[k, :WIDTH] = x_ref[:, pl.ds(pl.multiple_of(k * TILE, TILE), TILE)].astype(F32)
        return 0

    for i in range(CHUNKS):
        loads[i].wait()
        lax.fori_loop(i * NS // CHUNKS, (i + 1) * NS // CHUNKS, fill, 0, unroll=8)
    for f in range(WIDTH):
        turned[f] = wide[:, f].T.astype(BF16)
    for load in loads[CHUNKS:]:
        load.wait()

    pl.semaphore_wait(barrier, 3 * (N - 1))

    @pl.when(b == rep)
    def _():
        mean_weight = wn_ref[...].astype(F32)
        weights = jnp.concatenate([ws_ref[...].astype(F32), mean_weight[8:], mean_weight[:8]], axis=0)
        wb[b] = jnp.concatenate([weights[:, :TILE], weights[:, TILE:]], axis=0).astype(BF16)
        each(lambda o: w_copy(o, b).start())

    def one_block(i, _):
        odd = i % 2
        away = odd * (4 - (i + 1) // 2) + (1 - odd) * (4 + i // 2)
        u = (b + away) % N
        gb[u] = gather_block(tiles_ref, wide, slot_ref, seed_ref, turned, rows, u)
        o = (u + N - b) % N

        @pl.when(o != 0)
        def _():
            x_copy(o, b).start()

        @pl.when(i == SPREAD)
        def _():
            @pl.when(b != rep)
            def _():
                w_copy((b + N - rep) % N, rep).wait_recv()

            each(lambda o: v_copy(o, rep).start())

        return 0

    lax.fori_loop(0, N, one_block, 0)
    xb[b] = gb[b]

    each(lambda o: v_copy(o, behind(rep, o)).wait_recv())
    w = wb[...].astype(F32)
    w = jnp.concatenate([w[:, :ROWS], w[:, ROWS:]], axis=2).reshape(N * ROWS, H).astype(BF16)
    each(lambda o: x_copy(o, behind(b, o)).wait_recv())
    x = xb[...].astype(F32)
    x = jnp.concatenate([x[:, ROWS * i:ROWS * (i + 1)] for i in range(3)], axis=2)
    x = x.reshape(N * ROWS, 3 * TILE).astype(BF16)
    part = lax.dot_general(x, w, (((0,), (0,)), ((), ())), preferred_element_type=F32)
    part = part.reshape(N, OWN, H)
    pf[...] = part
    ps[...] = part.astype(BF16)
    each(lambda o: p_copy(o, a).start())
    pr[a] = jnp.zeros((OWN, H), BF16)
    each(lambda o: p_copy(o, behind(a, o)).wait_recv())
    pre = pf[a] + jnp.sum(pr[...].astype(F32), axis=0)

    sigma = jax.nn.sigmoid(pre)
    db[a] = (dh_ref[...].astype(F32) * sigma * (1.0 + pre * (1.0 - sigma))).astype(BF16)
    each(lambda o: d_copy(o, a).start())
    hid_ref[...] = (pre * sigma).astype(BF16)
    each(lambda o: d_copy(o, behind(a, o)).wait_recv())

    d_pre = db[...].reshape(N * OWN, H)
    grad = jnp.dot(x, d_pre, preferred_element_type=F32).reshape(N, ROWS, H)
    grad = jnp.concatenate([grad[:, :, :TILE], grad[:, :, TILE:]], axis=1)
    qf[...] = grad
    qs[...] = grad.astype(BF16)
    each(lambda o: q_copy(o, b).start())
    qr[b] = jnp.zeros((2 * ROWS, TILE), BF16)
    each(lambda o: q_copy(o, behind(b, o)).wait_recv())
    mine = qf[b] + jnp.sum(qr[...].astype(F32), axis=0)

    es[...] = mine.astype(BF16)
    each(lambda o: e_copy(o, rep).start())
    er[rep] = mine.astype(BF16)
    each(lambda o: e_copy(o, behind(rep, o)).wait_recv())
    total = jnp.sum(er[...].astype(F32), axis=0)
    total = jnp.concatenate([total[:ROWS], total[ROWS:]], axis=1)
    gs_ref[...] = total[:WIDTH]
    gn_ref[:8] = total[16:]
    gn_ref[8:] = total[WIDTH:16]

    @pl.when(b == rep)
    def _():
        each(lambda o: w_copy(o, b).wait_send())

    each(lambda o: v_copy(o, rep).wait_send())
    each(lambda o: x_copy(o, b).wait_send())
    each(lambda o: p_copy(o, a).wait_send())
    each(lambda o: d_copy(o, a).wait_send())
    each(lambda o: q_copy(o, b).wait_send())
    each(lambda o: e_copy(o, rep).wait_send())


def local(features, w_self, w_neighbor, tile_list, nbr_slot, seed_ids, d_hidden):
    vmem = pl.BlockSpec(memory_space=pltpu.VMEM)
    dma = pltpu.SemaphoreType.DMA
    return pl.pallas_call(
        sage_kernel,
        out_shape=(
            jax.ShapeDtypeStruct((OWN, H), BF16),
            jax.ShapeDtypeStruct((WIDTH, H), F32),
            jax.ShapeDtypeStruct((WIDTH, H), F32),
        ),
        in_specs=[pl.BlockSpec(memory_space=pltpu.HBM)] * 7,
        out_specs=(vmem,) * 3,
        scratch_shapes=[
            pltpu.VMEM((WIDTH, NS * TILE), BF16),
            pltpu.SMEM((LISTED, TB), jnp.int32),
            pltpu.VMEM((FAN, TB * TILE), jnp.int32),
            pltpu.VMEM((TB, 1, TILE), jnp.int32),
            pltpu.VMEM((WIDTH, H), BF16),
            pltpu.VMEM((WIDTH, H), BF16),
            pltpu.VMEM((OWN, H), BF16),
            pltpu.VMEM((NS, 16, TILE), F32),
            pltpu.VMEM((WIDTH, TILE, NS), BF16),
            pltpu.VMEM((3 * ROWS, TILE), F32),
            pltpu.VMEM((N, BLOCK, TILE), BF16),
            pltpu.VMEM((N, BLOCK, TILE), BF16),
            pltpu.VMEM((N, 2 * ROWS, TILE), BF16),
            pltpu.VMEM((N, OWN, H), F32),
            pltpu.VMEM((N, OWN, H), BF16),
            pltpu.VMEM((N, OWN, H), BF16),
            pltpu.VMEM((N, OWN, H), BF16),
            pltpu.VMEM((N, 2 * ROWS, TILE), F32),
            pltpu.VMEM((N, 2 * ROWS, TILE), BF16),
            pltpu.VMEM((N, 2 * ROWS, TILE), BF16),
            pltpu.VMEM((2 * ROWS, TILE), BF16),
            pltpu.VMEM((N, 2 * ROWS, TILE), BF16),
        ]
        + [dma((CHUNKS + 6,))] + [dma((N,))] * 14,
        compiler_params=pltpu.CompilerParams(
            collective_id=0, has_side_effects=True, vmem_limit_bytes=63 * 2**20
        ),
        name="exchange",
    )(
        features[0], tile_list.T, nbr_slot.T, seed_ids.reshape(TB, 1, TILE), w_self, w_neighbor, d_hidden
    )


def solution(mesh):
    placed = (
        P("rep", "feat", None),
        P("feat", None),
        P("feat", None),
        P("rep", None),
        P("rep", None),
        P("rep"),
        P(("rep", "feat"), None),
    )
    return jax.shard_map(
        local,
        mesh=mesh,
        in_specs=placed,
        out_specs=(P(("rep", "feat"), None), P("feat", None), P("feat", None)),
        check_vma=False,
    )
```

```python
import jax
import jax.numpy as jnp
from jax import lax
from jax.experimental import pallas as pl
from jax.experimental.pallas import tpu as pltpu
from jax.sharding import PartitionSpec as P

MESH = pl.DeviceIdType.MESH
F32, BF16 = jnp.float32, jnp.bfloat16
N = 8
TILE, TB, FAN, LISTED, NS = 128, 24, 10, 16, 256
WIDTH = 12
ROWS = 2 * WIDTH
BLOCK = 80
OWN = 48
H = 256
CHUNKS = 4
AHEAD = 4


def lane_pick(values, lanes):
    return jnp.take_along_axis(values, lanes, axis=1, mode="promise_in_bounds")


def select_tree(level, bits):
    for bit in bits:
        level = [jnp.where(bit, level[i + 1], level[i]) for i in range(0, len(level), 2)]
    return level[0]


def neighbor_sums(tiles_ref, wide, slot_ref, t):
    low, high = [], []
    for k in range(LISTED):
        block = wide[tiles_ref[k, t]]
        low.append(block[:8])
        high.append(block[8:WIDTH])
    pairs = [jnp.concatenate(high[k:k + 2], axis=0) for k in range(0, LISTED, 2)]
    upper = lax.broadcasted_iota(jnp.int32, (8, TILE), 0) >= 4
    total_low = jnp.zeros((8, TILE), F32)
    total_pair = jnp.zeros((8, TILE), F32)
    targets = pl.ds(pl.multiple_of(t * TILE, TILE), TILE)
    for j in range(FAN):
        slot = jnp.broadcast_to(slot_ref[j:j + 1, targets], (8, TILE))
        lane = slot & (TILE - 1)
        bits = [(slot & (TILE << b)) != 0 for b in range(4)]
        total_low += select_tree([lane_pick(v, lane) for v in low], bits)
        picked = select_tree([lane_pick(v, lane) for v in pairs], bits[1:])
        total_pair += jnp.where(bits[0] == upper, picked, 0.0)
    return total_low, total_pair[:4] + total_pair[4:]


def gather_block(tiles_ref, wide, slot_ref, seed_ref, turned, rows, u):
    span = 3 * TILE
    seed = jnp.concatenate([seed_ref[3 * u + i] for i in range(3)], axis=1)
    hot = (lax.broadcasted_iota(jnp.int32, (NS, span), 0) == (seed >> 7)).astype(F32).astype(BF16)
    mask = lax.broadcasted_iota(jnp.int32, (TILE, span), 0) == (seed & (TILE - 1))
    for f in range(WIDTH):
        columns = jnp.dot(turned[f], hot, preferred_element_type=F32)
        row = jnp.sum(jnp.where(mask, columns, 0.0), axis=0, keepdims=True)
        for i in range(3):
            rows[ROWS * i + f:ROWS * i + f + 1] = row[:, i * TILE:(i + 1) * TILE]
    for i in range(3):
        low, high = neighbor_sums(tiles_ref, wide, slot_ref, 3 * u + i)
        rows[ROWS * i + WIDTH:ROWS * i + 16] = high * (1.0 / FAN)
        rows[ROWS * i + 16:ROWS * (i + 1)] = low * (1.0 / FAN)
    return jnp.concatenate([rows[...], jnp.zeros((BLOCK - 3 * ROWS, TILE), F32)], axis=0).astype(BF16)


def sage_kernel(
    x_hbm, tiles_hbm, slot_hbm, seed_hbm, ws_hbm, wn_hbm, dh_hbm, hid_ref, gs_ref, gn_ref,
    x_ref, tiles_ref, slot_ref, seed_ref, ws_ref, wn_ref, dh_ref, wide, turned, rows, gb,
    xb, wb, pf, ps, pr, db, qf, qs, qr, es, er,
    l_in, x_out, x_in, w_out, w_in, v_out, v_in, p_out, p_in, d_out, d_in, q_out, q_in, e_out, e_in,
):
    rep = lax.axis_index("rep")
    feat = lax.axis_index("feat")
    b, a = feat // N, feat % N
    chunk = NS * TILE // CHUNKS

    pairs = [
        (x_hbm.at[:, pl.ds(i * chunk, chunk)], x_ref.at[:, pl.ds(i * chunk, chunk)]) for i in range(CHUNKS)
    ] + [
        (tiles_hbm, tiles_ref), (slot_hbm, slot_ref), (seed_hbm, seed_ref),
        (ws_hbm, ws_ref), (wn_hbm, wn_ref), (dh_hbm, dh_ref),
    ]
    loads = [pltpu.make_async_copy(src, dst, l_in.at[i]) for i, (src, dst) in enumerate(pairs)]
    for load in loads:
        load.start()

    def ahead(place, o):
        return lax.rem(place + o, N)

    def behind(place, o):
        return lax.rem(place + N - o, N)

    def along_b(o):
        return rep, ahead(b, o) * N + a

    def along_a(o):
        return rep, b * N + ahead(a, o)

    def along_rep(o):
        return ahead(rep, o), feat

    barrier = pltpu.get_barrier_semaphore()

    def each(body):
        def step(o, _):
            body(o)
            return 0
        lax.fori_loop(1, N, step, 0)

    def greet(way):
        return lambda o: pl.semaphore_signal(barrier, inc=1, device_id=way(o), device_id_type=MESH)

    each(greet(along_b))
    each(greet(along_a))
    each(greet(along_rep))

    def copy(src, dst, out_sem, in_sem, o, target):
        return pltpu.make_async_remote_copy(
            src_ref=src, dst_ref=dst, send_sem=out_sem.at[o], recv_sem=in_sem.at[o],
            device_id=target, device_id_type=MESH,
        )

    def x_copy(o, slot):
        return copy(gb.at[ahead(b, o)], xb.at[slot], x_out, x_in, o, along_b(o))

    def w_copy(o, slot):
        return copy(wb.at[b], wb.at[slot], w_out, w_in, o, along_b(o))

    def v_copy(o, slot):
        return copy(wb.at[rep], wb.at[slot], v_out, v_in, o, along_rep(o))

    def p_copy(o, slot):
        return copy(ps.at[ahead(a, o)], pr.at[slot], p_out, p_in, o, along_a(o))

    def d_copy(o, slot):
        return copy(db.at[a], db.at[slot], d_out, d_in, o, along_a(o))

    def q_copy(o, slot):
        return copy(qs.at[ahead(b, o)], qr.at[slot], q_out, q_in, o, along_b(o))

    def e_copy(o, slot):
        return copy(es, er.at[slot], e_out, e_in, o, along_rep(o))

    def fill(k, _):
        wide[k, :WIDTH] = x_ref[:, pl.ds(pl.multiple_of(k * TILE, TILE), TILE)].astype(F32)
        return 0

    for i in range(CHUNKS):
        loads[i].wait()
        lax.fori_loop(i * NS // CHUNKS, (i + 1) * NS // CHUNKS, fill, 0, unroll=8)
    for f in range(WIDTH):
        turned[f] = wide[:, f].T.astype(BF16)
    for load in loads[CHUNKS:]:
        load.wait()

    @pl.when(b == rep)
    def _():
        mean_weight = wn_ref[...].astype(F32)
        weights = jnp.concatenate([ws_ref[...].astype(F32), mean_weight[8:], mean_weight[:8]], axis=0)
        wb[b] = jnp.concatenate([weights[:, :TILE], weights[:, TILE:]], axis=0).astype(BF16)

    def block_at(i):
        odd = i % 2
        away = odd * (4 - (i + 1) // 2) + (1 - odd) * (4 + i // 2)
        return (b + away) % N

    def send_block(i):
        x_copy((block_at(i) + N - b) % N, b).start()

    def one_block(i, _):
        u = block_at(i)
        gb[u] = gather_block(tiles_ref, wide, slot_ref, seed_ref, turned, rows, u)

        @pl.when(i == AHEAD - 1)
        def _():
            pl.semaphore_wait(barrier, 3 * (N - 1))

            @pl.when(b == rep)
            def _():
                each(lambda o: w_copy(o, b).start())

            lax.fori_loop(0, AHEAD - 1, lambda k, _: (send_block(k), 0)[1], 0)

        @pl.when((i >= AHEAD - 1) & (i < N - 1))
        def _():
            send_block(i)

        return 0

    lax.fori_loop(0, N, one_block, 0)
    xb[b] = gb[b]

    @pl.when(b != rep)
    def _():
        w_copy((b + N - rep) % N, rep).wait_recv()

    each(lambda o: v_copy(o, rep).start())
    each(lambda o: v_copy(o, behind(rep, o)).wait_recv())
    w = wb[...].astype(F32)
    w = jnp.concatenate([w[:, :ROWS], w[:, ROWS:]], axis=2).reshape(N * ROWS, H).astype(BF16)
    each(lambda o: x_copy(o, behind(b, o)).wait_recv())
    x = xb[...].astype(F32)
    x = jnp.concatenate([x[:, ROWS * i:ROWS * (i + 1)] for i in range(3)], axis=2)
    x = x.reshape(N * ROWS, 3 * TILE).astype(BF16)
    part = lax.dot_general(x, w, (((0,), (0,)), ((), ())), preferred_element_type=F32)
    part = part.reshape(N, OWN, H)
    pf[...] = part
    ps[...] = part.astype(BF16)
    each(lambda o: p_copy(o, a).start())
    pr[a] = jnp.zeros((OWN, H), BF16)
    each(lambda o: p_copy(o, behind(a, o)).wait_recv())
    pre = pf[a] + jnp.sum(pr[...].astype(F32), axis=0)

    sigma = jax.nn.sigmoid(pre)
    db[a] = (dh_ref[...].astype(F32) * sigma * (1.0 + pre * (1.0 - sigma))).astype(BF16)
    each(lambda o: d_copy(o, a).start())
    hid_ref[...] = (pre * sigma).astype(BF16)
    each(lambda o: d_copy(o, behind(a, o)).wait_recv())

    d_pre = db[...].reshape(N * OWN, H)
    grad = jnp.dot(x, d_pre, preferred_element_type=F32).reshape(N, ROWS, H)
    grad = jnp.concatenate([grad[:, :, :TILE], grad[:, :, TILE:]], axis=1)
    qf[...] = grad
    qs[...] = grad.astype(BF16)
    each(lambda o: q_copy(o, b).start())
    qr[b] = jnp.zeros((2 * ROWS, TILE), BF16)
    each(lambda o: q_copy(o, behind(b, o)).wait_recv())
    mine = qf[b] + jnp.sum(qr[...].astype(F32), axis=0)

    es[...] = mine.astype(BF16)
    each(lambda o: e_copy(o, rep).start())
    er[rep] = mine.astype(BF16)
    each(lambda o: e_copy(o, behind(rep, o)).wait_recv())
    total = jnp.sum(er[...].astype(F32), axis=0)
    total = jnp.concatenate([total[:ROWS], total[ROWS:]], axis=1)
    gs_ref[...] = total[:WIDTH]
    gn_ref[:8] = total[16:]
    gn_ref[8:] = total[WIDTH:16]

    @pl.when(b == rep)
    def _():
        each(lambda o: w_copy(o, b).wait_send())

    each(lambda o: v_copy(o, rep).wait_send())
    each(lambda o: x_copy(o, b).wait_send())
    each(lambda o: p_copy(o, a).wait_send())
    each(lambda o: d_copy(o, a).wait_send())
    each(lambda o: q_copy(o, b).wait_send())
    each(lambda o: e_copy(o, rep).wait_send())


def write_kernel(hid_in, gs_in, gn_in, hid_out, gs_out, gn_out):
    hid_out[...] = hid_in[...]
    gs_out[...] = gs_in[...]
    gn_out[...] = gn_in[...]


def local(features, w_self, w_neighbor, tile_list, nbr_slot, seed_ids, d_hidden):
    vmem = pl.BlockSpec(memory_space=pltpu.VMEM)
    dma = pltpu.SemaphoreType.DMA
    results = pl.pallas_call(
        sage_kernel,
        out_shape=(
            jax.ShapeDtypeStruct((OWN, H), BF16),
            jax.ShapeDtypeStruct((WIDTH, H), F32),
            jax.ShapeDtypeStruct((WIDTH, H), F32),
        ),
        in_specs=[pl.BlockSpec(memory_space=pltpu.HBM)] * 7,
        out_specs=(vmem,) * 3,
        scratch_shapes=[
            pltpu.VMEM((WIDTH, NS * TILE), BF16),
            pltpu.SMEM((LISTED, TB), jnp.int32),
            pltpu.VMEM((FAN, TB * TILE), jnp.int32),
            pltpu.VMEM((TB, 1, TILE), jnp.int32),
            pltpu.VMEM((WIDTH, H), BF16),
            pltpu.VMEM((WIDTH, H), BF16),
            pltpu.VMEM((OWN, H), BF16),
            pltpu.VMEM((NS, 16, TILE), F32),
            pltpu.VMEM((WIDTH, TILE, NS), BF16),
            pltpu.VMEM((3 * ROWS, TILE), F32),
            pltpu.VMEM((N, BLOCK, TILE), BF16),
            pltpu.VMEM((N, BLOCK, TILE), BF16),
            pltpu.VMEM((N, 2 * ROWS, TILE), BF16),
            pltpu.VMEM((N, OWN, H), F32),
            pltpu.VMEM((N, OWN, H), BF16),
            pltpu.VMEM((N, OWN, H), BF16),
            pltpu.VMEM((N, OWN, H), BF16),
            pltpu.VMEM((N, 2 * ROWS, TILE), F32),
            pltpu.VMEM((N, 2 * ROWS, TILE), BF16),
            pltpu.VMEM((N, 2 * ROWS, TILE), BF16),
            pltpu.VMEM((2 * ROWS, TILE), BF16),
            pltpu.VMEM((N, 2 * ROWS, TILE), BF16),
        ]
        + [dma((CHUNKS + 6,))] + [dma((N,))] * 14,
        compiler_params=pltpu.CompilerParams(
            collective_id=0, has_side_effects=True, vmem_limit_bytes=63 * 2**20
        ),
        name="exchange",
    )(
        features[0], tile_list.T, nbr_slot.T, seed_ids.reshape(TB, 1, TILE), w_self, w_neighbor, d_hidden
    )
    return pl.pallas_call(
        write_kernel,
        out_shape=tuple(jax.ShapeDtypeStruct(r.shape, r.dtype) for r in results),
        in_specs=[vmem] * 3,
        out_specs=(vmem,) * 3,
        name="write",
    )(*results)


def solution(mesh):
    placed = (
        P("rep", "feat", None),
        P("feat", None),
        P("feat", None),
        P("rep", None),
        P("rep", None),
        P("rep"),
        P(("rep", "feat"), None),
    )
    return jax.shard_map(
        local,
        mesh=mesh,
        in_specs=placed,
        out_specs=(P(("rep", "feat"), None), P("feat", None), P("feat", None)),
        check_vma=False,
    )
```

```python
import jax
import jax.numpy as jnp
from jax import lax
from jax.experimental import pallas as pl
from jax.experimental.pallas import tpu as pltpu
from jax.sharding import PartitionSpec as P

MESH = pl.DeviceIdType.MESH
F32, BF16 = jnp.float32, jnp.bfloat16
N = 8
TILE, TB, FAN, LISTED, NS = 128, 24, 10, 16, 256
WIDTH = 12
ROWS = 2 * WIDTH
BLOCK = 80
OWN = 48
H = 256
CHUNKS = 4
AHEAD = 4


def lane_pick(values, lanes):
    return jnp.take_along_axis(values, lanes, axis=1, mode="promise_in_bounds")


def select_tree(level, bits):
    for bit in bits:
        level = [jnp.where(bit, level[i + 1], level[i]) for i in range(0, len(level), 2)]
    return level[0]


def neighbor_sums(tiles_ref, wide, slot_ref, t):
    low, high = [], []
    for k in range(LISTED):
        block = wide[tiles_ref[k, t]]
        low.append(block[:8])
        high.append(block[8:WIDTH])
    pairs = [jnp.concatenate(high[k:k + 2], axis=0) for k in range(0, LISTED, 2)]
    upper = lax.broadcasted_iota(jnp.int32, (8, TILE), 0) >= 4
    total_low = jnp.zeros((8, TILE), F32)
    total_pair = jnp.zeros((8, TILE), F32)
    targets = pl.ds(pl.multiple_of(t * TILE, TILE), TILE)
    for j in range(FAN):
        slot = jnp.broadcast_to(slot_ref[j:j + 1, targets], (8, TILE))
        lane = slot & (TILE - 1)
        bits = [(slot & (TILE << b)) != 0 for b in range(4)]
        total_low += select_tree([lane_pick(v, lane) for v in low], bits)
        picked = select_tree([lane_pick(v, lane) for v in pairs], bits[1:])
        total_pair += jnp.where(bits[0] == upper, picked, 0.0)
    return total_low, total_pair[:4] + total_pair[4:]


def gather_block(tiles_ref, wide, slot_ref, seed_ref, turned, rows, u):
    span = 3 * TILE
    seed = jnp.concatenate([seed_ref[3 * u + i] for i in range(3)], axis=1)
    hot = (lax.broadcasted_iota(jnp.int32, (NS, span), 0) == (seed >> 7)).astype(F32).astype(BF16)
    mask = lax.broadcasted_iota(jnp.int32, (TILE, span), 0) == (seed & (TILE - 1))
    for f in range(WIDTH):
        columns = jnp.dot(turned[f], hot, preferred_element_type=F32)
        row = jnp.sum(jnp.where(mask, columns, 0.0), axis=0, keepdims=True)
        for i in range(3):
            rows[ROWS * i + f:ROWS * i + f + 1] = row[:, i * TILE:(i + 1) * TILE]
    for i in range(3):
        low, high = neighbor_sums(tiles_ref, wide, slot_ref, 3 * u + i)
        rows[ROWS * i + WIDTH:ROWS * i + 16] = high * (1.0 / FAN)
        rows[ROWS * i + 16:ROWS * (i + 1)] = low * (1.0 / FAN)
    return jnp.concatenate([rows[...], jnp.zeros((BLOCK - 3 * ROWS, TILE), F32)], axis=0).astype(BF16)


def sage_kernel(
    x_hbm, tiles_hbm, slot_hbm, seed_hbm, ws_hbm, wn_hbm, dh_hbm, hid_ref, gs_ref, gn_ref,
    x_ref, tiles_ref, slot_ref, seed_ref, ws_ref, wn_ref, dh_ref, wide, turned, rows, gb,
    xb, wb, pf, ps, pr, db, qf, qs, qr, es, er,
    l_in, x_out, x_in, w_out, w_in, v_out, v_in, p_out, p_in, d_out, d_in, q_out, q_in, e_out, e_in,
):
    rep = lax.axis_index("rep")
    feat = lax.axis_index("feat")
    b, a = feat // N, feat % N
    chunk = NS * TILE // CHUNKS

    pairs = [
        (x_hbm.at[:, pl.ds(i * chunk, chunk)], x_ref.at[:, pl.ds(i * chunk, chunk)]) for i in range(CHUNKS)
    ] + [
        (tiles_hbm, tiles_ref), (slot_hbm, slot_ref), (seed_hbm, seed_ref),
        (ws_hbm, ws_ref), (wn_hbm, wn_ref), (dh_hbm, dh_ref),
    ]
    loads = [pltpu.make_async_copy(src, dst, l_in.at[i]) for i, (src, dst) in enumerate(pairs)]
    for load in loads:
        load.start()

    def ahead(place, o):
        return lax.rem(place + o, N)

    def behind(place, o):
        return lax.rem(place + N - o, N)

    def along_b(o):
        return rep, ahead(b, o) * N + a

    def along_a(o):
        return rep, b * N + ahead(a, o)

    def along_rep(o):
        return ahead(rep, o), feat

    barrier = pltpu.get_barrier_semaphore()

    def each(body, order=(4, 3, 5, 2, 6, 1, 7)):
        for o in order:
            body(o)

    def greet(way):
        return lambda o: pl.semaphore_signal(barrier, inc=1, device_id=way(o), device_id_type=MESH)

    each(greet(along_b))
    each(greet(along_a))
    each(greet(along_rep))

    def copy(src, dst, out_sem, in_sem, o, target):
        return pltpu.make_async_remote_copy(
            src_ref=src, dst_ref=dst, send_sem=out_sem.at[o], recv_sem=in_sem.at[o],
            device_id=target, device_id_type=MESH,
        )

    def x_copy(o, slot):
        return copy(gb.at[ahead(b, o)], xb.at[slot], x_out, x_in, o, along_b(o))

    def w_copy(o, slot):
        return copy(wb.at[b], wb.at[slot], w_out, w_in, o, along_b(o))

    def v_copy(o, slot):
        return copy(wb.at[rep], wb.at[slot], v_out, v_in, o, along_rep(o))

    def p_copy(o, slot):
        return copy(ps.at[ahead(a, o)], pr.at[slot], p_out, p_in, o, along_a(o))

    def d_copy(o, slot):
        return copy(db.at[a], db.at[slot], d_out, d_in, o, along_a(o))

    def q_copy(o, slot):
        return copy(qs.at[ahead(b, o)], qr.at[slot], q_out, q_in, o, along_b(o))

    def e_copy(o, slot):
        return copy(es, er.at[slot], e_out, e_in, o, along_rep(o))

    def fill(k, _):
        wide[k, :WIDTH] = x_ref[:, pl.ds(pl.multiple_of(k * TILE, TILE), TILE)].astype(F32)
        return 0

    for i in range(CHUNKS):
        loads[i].wait()
        lax.fori_loop(i * NS // CHUNKS, (i + 1) * NS // CHUNKS, fill, 0, unroll=8)
    for f in range(WIDTH):
        turned[f] = wide[:, f].T.astype(BF16)
    for load in loads[CHUNKS:]:
        load.wait()

    @pl.when(b == rep)
    def _():
        mean_weight = wn_ref[...].astype(F32)
        weights = jnp.concatenate([ws_ref[...].astype(F32), mean_weight[8:], mean_weight[:8]], axis=0)
        wb[b] = jnp.concatenate([weights[:, :TILE], weights[:, TILE:]], axis=0).astype(BF16)

    def block_at(i):
        odd = i % 2
        away = odd * (4 - (i + 1) // 2) + (1 - odd) * (4 + i // 2)
        return (b + away) % N

    def send_block(i):
        x_copy((block_at(i) + N - b) % N, b).start()

    def one_block(i, _):
        u = block_at(i)
        gb[u] = gather_block(tiles_ref, wide, slot_ref, seed_ref, turned, rows, u)

        @pl.when(i == AHEAD - 1)
        def _():
            pl.semaphore_wait(barrier, 3 * (N - 1))

            @pl.when(b == rep)
            def _():
                each(lambda o: w_copy(o, b).start())

            lax.fori_loop(0, AHEAD - 1, lambda k, _: (send_block(k), 0)[1], 0)

        @pl.when((i >= AHEAD - 1) & (i < N - 1))
        def _():
            send_block(i)

        return 0

    lax.fori_loop(0, N, one_block, 0)
    xb[b] = gb[b]

    @pl.when(b != rep)
    def _():
        w_copy((b + N - rep) % N, rep).wait_recv()

    each(lambda o: v_copy(o, rep).start())
    each(lambda o: v_copy(o, behind(rep, o)).wait_recv())
    w = wb[...].astype(F32)
    w = jnp.concatenate([w[:, :ROWS], w[:, ROWS:]], axis=2).reshape(N * ROWS, H).astype(BF16)
    each(lambda o: x_copy(o, behind(b, o)).wait_recv())
    x = xb[...].astype(F32)
    x = jnp.concatenate([x[:, ROWS * i:ROWS * (i + 1)] for i in range(3)], axis=2)
    x = x.reshape(N * ROWS, 3 * TILE).astype(BF16)
    part = lax.dot_general(x, w, (((0,), (0,)), ((), ())), preferred_element_type=F32)
    part = part.reshape(N, OWN, H)
    pf[...] = part
    ps[...] = part.astype(BF16)
    each(lambda o: p_copy(o, a).start(), (2, 6, 1, 3, 5, 7, 4))
    pr[a] = jnp.zeros((OWN, H), BF16)
    each(lambda o: p_copy(o, behind(a, o)).wait_recv())
    pre = pf[a] + jnp.sum(pr[...].astype(F32), axis=0)

    sigma = jax.nn.sigmoid(pre)
    db[a] = (dh_ref[...].astype(F32) * sigma * (1.0 + pre * (1.0 - sigma))).astype(BF16)
    each(lambda o: d_copy(o, a).start(), (2, 6, 1, 3, 5, 7, 4))
    hid_ref[...] = (pre * sigma).astype(BF16)
    each(lambda o: d_copy(o, behind(a, o)).wait_recv())

    d_pre = db[...].reshape(N * OWN, H)
    grad = jnp.dot(x, d_pre, preferred_element_type=F32).reshape(N, ROWS, H)
    grad = jnp.concatenate([grad[:, :, :TILE], grad[:, :, TILE:]], axis=1)
    qf[...] = grad
    qs[...] = grad.astype(BF16)
    each(lambda o: q_copy(o, b).start())
    qr[b] = jnp.zeros((2 * ROWS, TILE), BF16)
    each(lambda o: q_copy(o, behind(b, o)).wait_recv())
    mine = qf[b] + jnp.sum(qr[...].astype(F32), axis=0)

    es[...] = mine.astype(BF16)
    each(lambda o: e_copy(o, rep).start())
    er[rep] = mine.astype(BF16)
    each(lambda o: e_copy(o, behind(rep, o)).wait_recv())
    total = jnp.sum(er[...].astype(F32), axis=0)
    total = jnp.concatenate([total[:ROWS], total[ROWS:]], axis=1)
    gs_ref[...] = total[:WIDTH]
    gn_ref[:8] = total[16:]
    gn_ref[8:] = total[WIDTH:16]

    @pl.when(b == rep)
    def _():
        each(lambda o: w_copy(o, b).wait_send())

    each(lambda o: v_copy(o, rep).wait_send())
    each(lambda o: x_copy(o, b).wait_send())
    each(lambda o: p_copy(o, a).wait_send())
    each(lambda o: d_copy(o, a).wait_send())
    each(lambda o: q_copy(o, b).wait_send())
    each(lambda o: e_copy(o, rep).wait_send())


def write_kernel(hid_in, gs_in, gn_in, hid_out, gs_out, gn_out):
    hid_out[...] = hid_in[...]
    gs_out[...] = gs_in[...]
    gn_out[...] = gn_in[...]


def local(features, w_self, w_neighbor, tile_list, nbr_slot, seed_ids, d_hidden):
    vmem = pl.BlockSpec(memory_space=pltpu.VMEM)
    dma = pltpu.SemaphoreType.DMA
    results = pl.pallas_call(
        sage_kernel,
        out_shape=(
            jax.ShapeDtypeStruct((OWN, H), BF16),
            jax.ShapeDtypeStruct((WIDTH, H), F32),
            jax.ShapeDtypeStruct((WIDTH, H), F32),
        ),
        in_specs=[pl.BlockSpec(memory_space=pltpu.HBM)] * 7,
        out_specs=(vmem,) * 3,
        scratch_shapes=[
            pltpu.VMEM((WIDTH, NS * TILE), BF16),
            pltpu.SMEM((LISTED, TB), jnp.int32),
            pltpu.VMEM((FAN, TB * TILE), jnp.int32),
            pltpu.VMEM((TB, 1, TILE), jnp.int32),
            pltpu.VMEM((WIDTH, H), BF16),
            pltpu.VMEM((WIDTH, H), BF16),
            pltpu.VMEM((OWN, H), BF16),
            pltpu.VMEM((NS, 16, TILE), F32),
            pltpu.VMEM((WIDTH, TILE, NS), BF16),
            pltpu.VMEM((3 * ROWS, TILE), F32),
            pltpu.VMEM((N, BLOCK, TILE), BF16),
            pltpu.VMEM((N, BLOCK, TILE), BF16),
            pltpu.VMEM((N, 2 * ROWS, TILE), BF16),
            pltpu.VMEM((N, OWN, H), F32),
            pltpu.VMEM((N, OWN, H), BF16),
            pltpu.VMEM((N, OWN, H), BF16),
            pltpu.VMEM((N, OWN, H), BF16),
            pltpu.VMEM((N, 2 * ROWS, TILE), F32),
            pltpu.VMEM((N, 2 * ROWS, TILE), BF16),
            pltpu.VMEM((N, 2 * ROWS, TILE), BF16),
            pltpu.VMEM((2 * ROWS, TILE), BF16),
            pltpu.VMEM((N, 2 * ROWS, TILE), BF16),
        ]
        + [dma((CHUNKS + 6,))] + [dma((N,))] * 14,
        compiler_params=pltpu.CompilerParams(
            collective_id=0, has_side_effects=True, vmem_limit_bytes=63 * 2**20
        ),
        name="exchange",
    )(
        features[0], tile_list.T, nbr_slot.T, seed_ids.reshape(TB, 1, TILE), w_self, w_neighbor, d_hidden
    )
    return pl.pallas_call(
        write_kernel,
        out_shape=tuple(jax.ShapeDtypeStruct(r.shape, r.dtype) for r in results),
        in_specs=[vmem] * 3,
        out_specs=(vmem,) * 3,
        name="write",
    )(*results)


def solution(mesh):
    placed = (
        P("rep", "feat", None),
        P("feat", None),
        P("feat", None),
        P("rep", None),
        P("rep", None),
        P("rep"),
        P(("rep", "feat"), None),
    )
    return jax.shard_map(
        local,
        mesh=mesh,
        in_specs=placed,
        out_specs=(P(("rep", "feat"), None), P("feat", None), P("feat", None)),
        check_vma=False,
    )
```

```python
import jax
import jax.numpy as jnp
from jax import lax
from jax.experimental import pallas as pl
from jax.experimental.pallas import tpu as pltpu
from jax.sharding import PartitionSpec as P

MESH = pl.DeviceIdType.MESH
F32, BF16 = jnp.float32, jnp.bfloat16
N = 8
TILE, TB, FAN, LISTED, NS = 128, 24, 10, 16, 256
WIDTH = 12
ROWS = 2 * WIDTH
BLOCK = 80
OWN = 48
H = 256
CHUNKS = 4
AHEAD = 4


def lane_pick(values, lanes):
    return jnp.take_along_axis(values, lanes, axis=1, mode="promise_in_bounds")


def select_tree(level, bits):
    for bit in bits:
        level = [jnp.where(bit, level[i + 1], level[i]) for i in range(0, len(level), 2)]
    return level[0]


def neighbor_sums(tiles_ref, wide, slot_ref, t):
    low, high = [], []
    for k in range(LISTED):
        block = wide[tiles_ref[k, t]]
        low.append(block[:8])
        high.append(block[8:WIDTH])
    pairs = [jnp.concatenate(high[k:k + 2], axis=0) for k in range(0, LISTED, 2)]
    upper = lax.broadcasted_iota(jnp.int32, (8, TILE), 0) >= 4
    total_low = jnp.zeros((8, TILE), F32)
    total_pair = jnp.zeros((8, TILE), F32)
    targets = pl.ds(pl.multiple_of(t * TILE, TILE), TILE)
    for j in range(FAN):
        slot = jnp.broadcast_to(slot_ref[j:j + 1, targets], (8, TILE))
        lane = slot & (TILE - 1)
        bits = [(slot & (TILE << b)) != 0 for b in range(4)]
        total_low += select_tree([lane_pick(v, lane) for v in low], bits)
        picked = select_tree([lane_pick(v, lane) for v in pairs], bits[1:])
        total_pair += jnp.where(bits[0] == upper, picked, 0.0)
    return total_low, total_pair[:4] + total_pair[4:]


def gather_block(tiles_ref, wide, slot_ref, seed_ref, turned, rows, u):
    span = 3 * TILE
    seed = jnp.concatenate([seed_ref[3 * u + i] for i in range(3)], axis=1)
    hot = (lax.broadcasted_iota(jnp.int32, (NS, span), 0) == (seed >> 7)).astype(F32).astype(BF16)
    mask = lax.broadcasted_iota(jnp.int32, (TILE, span), 0) == (seed & (TILE - 1))
    for f in range(WIDTH):
        columns = jnp.dot(turned[f], hot, preferred_element_type=F32)
        row = jnp.sum(jnp.where(mask, columns, 0.0), axis=0, keepdims=True)
        for i in range(3):
            rows[ROWS * i + f:ROWS * i + f + 1] = row[:, i * TILE:(i + 1) * TILE]
    for i in range(3):
        low, high = neighbor_sums(tiles_ref, wide, slot_ref, 3 * u + i)
        rows[ROWS * i + WIDTH:ROWS * i + 16] = high * (1.0 / FAN)
        rows[ROWS * i + 16:ROWS * (i + 1)] = low * (1.0 / FAN)
    return jnp.concatenate([rows[...], jnp.zeros((BLOCK - 3 * ROWS, TILE), F32)], axis=0).astype(BF16)


def sage_kernel(
    x_hbm, tiles_hbm, slot_hbm, seed_hbm, ws_hbm, wn_hbm, dh_hbm, hid_ref, gs_ref, gn_ref,
    x_ref, tiles_ref, slot_ref, seed_ref, ws_ref, wn_ref, dh_ref, wide, turned, rows, gb,
    xb, wb, pf, ps, pr, db, qf, qs, qr, es, er,
    l_in, x_out, x_in, w_out, w_in, v_out, v_in, p_out, p_in, d_out, d_in, q_out, q_in, e_out, e_in,
):
    rep = lax.axis_index("rep")
    feat = lax.axis_index("feat")
    b, a = feat // N, feat % N
    chunk = NS * TILE // CHUNKS

    pairs = [
        (x_hbm.at[:, pl.ds(i * chunk, chunk)], x_ref.at[:, pl.ds(i * chunk, chunk)]) for i in range(CHUNKS)
    ] + [
        (tiles_hbm, tiles_ref), (slot_hbm, slot_ref), (seed_hbm, seed_ref),
        (ws_hbm, ws_ref), (wn_hbm, wn_ref), (dh_hbm, dh_ref),
    ]
    loads = [pltpu.make_async_copy(src, dst, l_in.at[i]) for i, (src, dst) in enumerate(pairs)]
    def ahead(place, o):
        return lax.rem(place + o, N)

    def behind(place, o):
        return lax.rem(place + N - o, N)

    def along_b(o):
        return rep, ahead(b, o) * N + a

    def along_a(o):
        return rep, b * N + ahead(a, o)

    def along_rep(o):
        return ahead(rep, o), feat

    barrier = pltpu.get_barrier_semaphore()

    def each(body, order=(4, 3, 5, 2, 6, 1, 7)):
        for o in order:
            body(o)

    def greet(way):
        return lambda o: pl.semaphore_signal(barrier, inc=1, device_id=way(o), device_id_type=MESH)

    each(greet(along_b))
    each(greet(along_a))
    each(greet(along_rep))

    for load in loads:
        load.start()

    def copy(src, dst, out_sem, in_sem, o, target):
        return pltpu.make_async_remote_copy(
            src_ref=src, dst_ref=dst, send_sem=out_sem.at[o], recv_sem=in_sem.at[o],
            device_id=target, device_id_type=MESH,
        )

    def x_copy(o, slot):
        return copy(gb.at[ahead(b, o)], xb.at[slot], x_out, x_in, o, along_b(o))

    def w_copy(o, slot):
        return copy(wb.at[b], wb.at[slot], w_out, w_in, o, along_b(o))

    def v_copy(o, slot):
        return copy(wb.at[rep], wb.at[slot], v_out, v_in, o, along_rep(o))

    def p_copy(o, slot):
        return copy(ps.at[ahead(a, o)], pr.at[slot], p_out, p_in, o, along_a(o))

    def d_copy(o, slot):
        return copy(db.at[a], db.at[slot], d_out, d_in, o, along_a(o))

    def q_copy(o, slot):
        return copy(qs.at[ahead(b, o)], qr.at[slot], q_out, q_in, o, along_b(o))

    def e_copy(o, slot):
        return copy(es, er.at[slot], e_out, e_in, o, along_rep(o))

    def fill(k, _):
        wide[k, :WIDTH] = x_ref[:, pl.ds(pl.multiple_of(k * TILE, TILE), TILE)].astype(F32)
        return 0

    for i in range(CHUNKS):
        loads[i].wait()
        lax.fori_loop(i * NS // CHUNKS, (i + 1) * NS // CHUNKS, fill, 0, unroll=8)
    for f in range(WIDTH):
        turned[f] = wide[:, f].T.astype(BF16)
    for load in loads[CHUNKS:]:
        load.wait()

    @pl.when(b == rep)
    def _():
        mean_weight = wn_ref[...].astype(F32)
        weights = jnp.concatenate([ws_ref[...].astype(F32), mean_weight[8:], mean_weight[:8]], axis=0)
        wb[b] = jnp.concatenate([weights[:, :TILE], weights[:, TILE:]], axis=0).astype(BF16)

    def block_at(i):
        odd = i % 2
        away = odd * (4 - (i + 1) // 2) + (1 - odd) * (4 + i // 2)
        return (b + away) % N

    def send_block(i):
        x_copy((block_at(i) + N - b) % N, b).start()

    def one_block(i, _):
        u = block_at(i)
        gb[u] = gather_block(tiles_ref, wide, slot_ref, seed_ref, turned, rows, u)

        @pl.when(i == AHEAD - 1)
        def _():
            pl.semaphore_wait(barrier, 3 * (N - 1))

            @pl.when(b == rep)
            def _():
                each(lambda o: w_copy(o, b).start())

            for k in range(AHEAD - 1):
                send_block(k)

        @pl.when((i >= AHEAD - 1) & (i < N - 1))
        def _():
            send_block(i)

        return 0

    lax.fori_loop(0, N, one_block, 0)
    xb[b] = gb[b]

    @pl.when(b != rep)
    def _():
        w_copy((b + N - rep) % N, rep).wait_recv()

    each(lambda o: v_copy(o, rep).start())
    each(lambda o: v_copy(o, behind(rep, o)).wait_recv())
    w = wb[...].astype(F32)
    w = jnp.concatenate([w[:, :ROWS], w[:, ROWS:]], axis=2).reshape(N * ROWS, H).astype(BF16)
    each(lambda o: x_copy(o, behind(b, o)).wait_recv())
    x = xb[...].astype(F32)
    x = jnp.concatenate([x[:, ROWS * i:ROWS * (i + 1)] for i in range(3)], axis=2)
    x = x.reshape(N * ROWS, 3 * TILE).astype(BF16)
    part = lax.dot_general(x, w, (((0,), (0,)), ((), ())), preferred_element_type=F32)
    part = part.reshape(N, OWN, H)
    pf[...] = part
    ps[...] = part.astype(BF16)
    each(lambda o: p_copy(o, a).start(), (2, 6, 1, 3, 5, 7, 4))
    pr[a] = jnp.zeros((OWN, H), BF16)
    each(lambda o: p_copy(o, behind(a, o)).wait_recv())
    pre = pf[a] + jnp.sum(pr[...].astype(F32), axis=0)

    sigma = jax.nn.sigmoid(pre)
    db[a] = (dh_ref[...].astype(F32) * sigma * (1.0 + pre * (1.0 - sigma))).astype(BF16)
    each(lambda o: d_copy(o, a).start(), (2, 6, 1, 3, 5, 7, 4))
    hid_ref[...] = (pre * sigma).astype(BF16)
    each(lambda o: d_copy(o, behind(a, o)).wait_recv())

    d_pre = db[...].reshape(N * OWN, H)
    grad = jnp.dot(x, d_pre, preferred_element_type=F32).reshape(N, ROWS, H)
    grad = jnp.concatenate([grad[:, :, :TILE], grad[:, :, TILE:]], axis=1)
    qf[...] = grad
    qs[...] = grad.astype(BF16)
    each(lambda o: q_copy(o, b).start())
    qr[b] = jnp.zeros((2 * ROWS, TILE), BF16)
    each(lambda o: q_copy(o, behind(b, o)).wait_recv())
    mine = qf[b] + jnp.sum(qr[...].astype(F32), axis=0)

    es[...] = mine.astype(BF16)
    each(lambda o: e_copy(o, rep).start())
    er[rep] = mine.astype(BF16)
    each(lambda o: e_copy(o, behind(rep, o)).wait_recv())
    total = jnp.sum(er[...].astype(F32), axis=0)
    total = jnp.concatenate([total[:ROWS], total[ROWS:]], axis=1)
    gs_ref[...] = total[:WIDTH]
    gn_ref[:8] = total[16:]
    gn_ref[8:] = total[WIDTH:16]

    @pl.when(b == rep)
    def _():
        each(lambda o: w_copy(o, b).wait_send())

    each(lambda o: v_copy(o, rep).wait_send())
    each(lambda o: x_copy(o, b).wait_send())
    each(lambda o: p_copy(o, a).wait_send())
    each(lambda o: d_copy(o, a).wait_send())
    each(lambda o: q_copy(o, b).wait_send())
    each(lambda o: e_copy(o, rep).wait_send())


def write_kernel(hid_in, gs_in, gn_in, hid_out, gs_out, gn_out, hid, gs, gn, sems):
    moves = [(hid_in, hid, hid_out), (gs_in, gs, gs_out), (gn_in, gn, gn_out)]
    reads = [pltpu.make_async_copy(src, mid, sems.at[i]) for i, (src, mid, _) in enumerate(moves)]
    writes = [pltpu.make_async_copy(mid, dst, sems.at[3 + i]) for i, (_, mid, dst) in enumerate(moves)]
    for read in reads:
        read.start()
    for read, write in zip(reads, writes):
        read.wait()
        write.start()
    for write in writes:
        write.wait()


def local(features, w_self, w_neighbor, tile_list, nbr_slot, seed_ids, d_hidden):
    vmem = pl.BlockSpec(memory_space=pltpu.VMEM)
    dma = pltpu.SemaphoreType.DMA
    results = pl.pallas_call(
        sage_kernel,
        out_shape=(
            jax.ShapeDtypeStruct((OWN, H), BF16),
            jax.ShapeDtypeStruct((WIDTH, H), F32),
            jax.ShapeDtypeStruct((WIDTH, H), F32),
        ),
        in_specs=[pl.BlockSpec(memory_space=pltpu.HBM)] * 7,
        out_specs=(vmem,) * 3,
        scratch_shapes=[
            pltpu.VMEM((WIDTH, NS * TILE), BF16),
            pltpu.SMEM((LISTED, TB), jnp.int32),
            pltpu.VMEM((FAN, TB * TILE), jnp.int32),
            pltpu.VMEM((TB, 1, TILE), jnp.int32),
            pltpu.VMEM((WIDTH, H), BF16),
            pltpu.VMEM((WIDTH, H), BF16),
            pltpu.VMEM((OWN, H), BF16),
            pltpu.VMEM((NS, 16, TILE), F32),
            pltpu.VMEM((WIDTH, TILE, NS), BF16),
            pltpu.VMEM((3 * ROWS, TILE), F32),
            pltpu.VMEM((N, BLOCK, TILE), BF16),
            pltpu.VMEM((N, BLOCK, TILE), BF16),
            pltpu.VMEM((N, 2 * ROWS, TILE), BF16),
            pltpu.VMEM((N, OWN, H), F32),
            pltpu.VMEM((N, OWN, H), BF16),
            pltpu.VMEM((N, OWN, H), BF16),
            pltpu.VMEM((N, OWN, H), BF16),
            pltpu.VMEM((N, 2 * ROWS, TILE), F32),
            pltpu.VMEM((N, 2 * ROWS, TILE), BF16),
            pltpu.VMEM((N, 2 * ROWS, TILE), BF16),
            pltpu.VMEM((2 * ROWS, TILE), BF16),
            pltpu.VMEM((N, 2 * ROWS, TILE), BF16),
        ]
        + [dma((CHUNKS + 6,))] + [dma((N,))] * 14,
        compiler_params=pltpu.CompilerParams(
            collective_id=0, has_side_effects=True, vmem_limit_bytes=63 * 2**20
        ),
        name="exchange",
    )(
        features[0], tile_list.T, nbr_slot.T, seed_ids.reshape(TB, 1, TILE), w_self, w_neighbor, d_hidden
    )
    return pl.pallas_call(
        write_kernel,
        out_shape=tuple(jax.ShapeDtypeStruct(r.shape, r.dtype) for r in results),
        in_specs=[pl.BlockSpec(memory_space=pl.ANY)] * 3,
        out_specs=(pl.BlockSpec(memory_space=pl.ANY),) * 3,
        scratch_shapes=[pltpu.VMEM(r.shape, r.dtype) for r in results] + [dma((6,))],
        compiler_params=pltpu.CompilerParams(vmem_limit_bytes=63 * 2**20),
        name="write",
    )(*results)


def solution(mesh):
    placed = (
        P("rep", "feat", None),
        P("feat", None),
        P("feat", None),
        P("rep", None),
        P("rep", None),
        P("rep"),
        P(("rep", "feat"), None),
    )
    return jax.shard_map(
        local,
        mesh=mesh,
        in_specs=placed,
        out_specs=(P(("rep", "feat"), None), P("feat", None), P("feat", None)),
        check_vma=False,
    )
```

```python
import jax
import jax.numpy as jnp
from jax import lax
from jax.experimental import pallas as pl
from jax.experimental.pallas import tpu as pltpu
from jax.sharding import PartitionSpec as P

MESH = pl.DeviceIdType.MESH
F32, BF16 = jnp.float32, jnp.bfloat16
N = 8
TILE, TB, FAN, LISTED, NS = 128, 24, 10, 16, 256
WIDTH = 12
ROWS = 2 * WIDTH
BLOCK = 80
OWN = 48
H = 256
CHUNKS = 4
AHEAD = 4


def lane_pick(values, lanes):
    return jnp.take_along_axis(values, lanes, axis=1, mode="promise_in_bounds")


def select_tree(level, bits):
    for bit in bits:
        level = [jnp.where(bit, level[i + 1], level[i]) for i in range(0, len(level), 2)]
    return level[0]


def neighbor_sums(tiles_ref, wide, slot_ref, t):
    low, high = [], []
    for k in range(LISTED):
        block = wide[tiles_ref[k, t]]
        low.append(block[:8])
        high.append(block[8:WIDTH])
    pairs = [jnp.concatenate(high[k:k + 2], axis=0) for k in range(0, LISTED, 2)]
    upper = lax.broadcasted_iota(jnp.int32, (8, TILE), 0) >= 4
    total_low = jnp.zeros((8, TILE), F32)
    total_pair = jnp.zeros((8, TILE), F32)
    targets = pl.ds(pl.multiple_of(t * TILE, TILE), TILE)
    for j in range(FAN):
        slot = jnp.broadcast_to(slot_ref[j:j + 1, targets], (8, TILE))
        lane = slot & (TILE - 1)
        bits = [(slot & (TILE << b)) != 0 for b in range(4)]
        total_low += select_tree([lane_pick(v, lane) for v in low], bits)
        picked = select_tree([lane_pick(v, lane) for v in pairs], bits[1:])
        total_pair += jnp.where(bits[0] == upper, picked, 0.0)
    return total_low, total_pair[:4] + total_pair[4:]


def gather_block(tiles_ref, wide, slot_ref, seed_ref, turned, rows, u):
    span = 3 * TILE
    seed = jnp.concatenate([seed_ref[3 * u + i] for i in range(3)], axis=1)
    hot = (lax.broadcasted_iota(jnp.int32, (NS, span), 0) == (seed >> 7)).astype(F32).astype(BF16)
    mask = lax.broadcasted_iota(jnp.int32, (TILE, span), 0) == (seed & (TILE - 1))
    for f in range(WIDTH):
        columns = jnp.dot(turned[f], hot, preferred_element_type=F32)
        row = jnp.sum(jnp.where(mask, columns, 0.0), axis=0, keepdims=True)
        for i in range(3):
            rows[ROWS * i + f:ROWS * i + f + 1] = row[:, i * TILE:(i + 1) * TILE]
    for i in range(3):
        low, high = neighbor_sums(tiles_ref, wide, slot_ref, 3 * u + i)
        rows[ROWS * i + WIDTH:ROWS * i + 16] = high * (1.0 / FAN)
        rows[ROWS * i + 16:ROWS * (i + 1)] = low * (1.0 / FAN)
    return jnp.concatenate([rows[...], jnp.zeros((BLOCK - 3 * ROWS, TILE), F32)], axis=0).astype(BF16)


def sage_kernel(
    x_hbm, tiles_hbm, slot_hbm, seed_hbm, ws_hbm, wn_hbm, dh_hbm, hid_ref, gs_ref, gn_ref,
    x_ref, tiles_ref, slot_ref, seed_ref, ws_ref, wn_ref, dh_ref, wide, turned, rows, gb,
    xb, wb, pf, ps, pr, db, qf, qs, qr, es, er,
    l_in, x_out, x_in, w_out, w_in, v_out, v_in, p_out, p_in, d_out, d_in, q_out, q_in, e_out, e_in,
):
    rep = lax.axis_index("rep")
    feat = lax.axis_index("feat")
    b, a = feat // N, feat % N
    chunk = NS * TILE // CHUNKS

    pairs = [
        (x_hbm.at[:, pl.ds(i * chunk, chunk)], x_ref.at[:, pl.ds(i * chunk, chunk)]) for i in range(CHUNKS)
    ] + [
        (tiles_hbm, tiles_ref), (slot_hbm, slot_ref), (seed_hbm, seed_ref),
        (ws_hbm, ws_ref), (wn_hbm, wn_ref), (dh_hbm, dh_ref),
    ]
    loads = [pltpu.make_async_copy(src, dst, l_in.at[i]) for i, (src, dst) in enumerate(pairs)]
    def ahead(place, o):
        return lax.rem(place + o, N)

    def behind(place, o):
        return lax.rem(place + N - o, N)

    def along_b(o):
        return rep, ahead(b, o) * N + a

    def along_a(o):
        return rep, b * N + ahead(a, o)

    def along_rep(o):
        return ahead(rep, o), feat

    barrier = pltpu.get_barrier_semaphore()

    def each(body, order=(4, 3, 5, 2, 6, 1, 7)):
        for o in order:
            body(o)

    def greet(way):
        return lambda o: pl.semaphore_signal(barrier, inc=1, device_id=way(o), device_id_type=MESH)

    each(greet(along_b))
    each(greet(along_a))
    each(greet(along_rep))

    for load in loads:
        load.start()

    def copy(src, dst, out_sem, in_sem, o, target):
        return pltpu.make_async_remote_copy(
            src_ref=src, dst_ref=dst, send_sem=out_sem.at[o], recv_sem=in_sem.at[o],
            device_id=target, device_id_type=MESH,
        )

    def x_copy(o, slot):
        return copy(gb.at[ahead(b, o)], xb.at[slot], x_out, x_in, o, along_b(o))

    def w_copy(o, slot):
        return copy(wb.at[b], wb.at[slot], w_out, w_in, o, along_b(o))

    def v_copy(o, slot):
        return copy(wb.at[rep], wb.at[slot], v_out, v_in, o, along_rep(o))

    def p_copy(o, slot):
        return copy(ps.at[ahead(a, o)], pr.at[slot], p_out, p_in, o, along_a(o))

    def d_copy(o, slot):
        return copy(db.at[a], db.at[slot], d_out, d_in, o, along_a(o))

    def q_copy(o, slot):
        return copy(qs.at[ahead(b, o)], qr.at[slot], q_out, q_in, o, along_b(o))

    def e_copy(o, slot):
        return copy(es, er.at[slot], e_out, e_in, o, along_rep(o))

    def fill(k, _):
        wide[k, :WIDTH] = x_ref[:, pl.ds(pl.multiple_of(k * TILE, TILE), TILE)].astype(F32)
        return 0

    for i in range(CHUNKS):
        loads[i].wait()
        lax.fori_loop(i * NS // CHUNKS, (i + 1) * NS // CHUNKS, fill, 0, unroll=8)
    for f in range(WIDTH):
        turned[f] = wide[:, f].T.astype(BF16)
    for load in loads[CHUNKS:]:
        load.wait()

    @pl.when(b == rep)
    def _():
        mean_weight = wn_ref[...].astype(F32)
        weights = jnp.concatenate([ws_ref[...].astype(F32), mean_weight[8:], mean_weight[:8]], axis=0)
        wb[b] = jnp.concatenate([weights[:, :TILE], weights[:, TILE:]], axis=0).astype(BF16)

    def block_at(i):
        odd = i % 2
        away = odd * (4 - (i + 1) // 2) + (1 - odd) * (4 + i // 2)
        return (b + away) % N

    def send_block(i):
        x_copy((block_at(i) + N - b) % N, b).start()

    def one_block(i, _):
        u = block_at(i)
        gb[u] = gather_block(tiles_ref, wide, slot_ref, seed_ref, turned, rows, u)

        @pl.when(i == AHEAD - 1)
        def _():
            pl.semaphore_wait(barrier, 3 * (N - 1))

            @pl.when(b == rep)
            def _():
                each(lambda o: w_copy(o, b).start())

            for k in range(AHEAD - 1):
                send_block(k)

        @pl.when((i >= AHEAD - 1) & (i < N - 1))
        def _():
            send_block(i)

        return 0

    lax.fori_loop(0, N, one_block, 0)
    xb[b] = gb[b]

    @pl.when(b != rep)
    def _():
        w_copy((b + N - rep) % N, rep).wait_recv()

    each(lambda o: v_copy(o, rep).start())
    each(lambda o: v_copy(o, behind(rep, o)).wait_recv())
    w = wb[...].astype(F32)
    w = jnp.concatenate([w[:, :ROWS], w[:, ROWS:]], axis=2).reshape(N * ROWS, H).astype(BF16)
    each(lambda o: x_copy(o, behind(b, o)).wait_recv())
    x = xb[...].astype(F32)
    x = jnp.concatenate([x[:, ROWS * i:ROWS * (i + 1)] for i in range(3)], axis=2)
    x = x.reshape(N * ROWS, 3 * TILE).astype(BF16)
    part = lax.dot_general(x, w, (((0,), (0,)), ((), ())), preferred_element_type=F32)
    part = part.reshape(N, OWN, H)
    pf[...] = part
    ps[...] = part.astype(BF16)
    each(lambda o: p_copy(o, a).start(), (2, 6, 1, 3, 5, 7, 4))
    pr[a] = jnp.zeros((OWN, H), BF16)
    each(lambda o: p_copy(o, behind(a, o)).wait_recv())
    pre = pf[a] + jnp.sum(pr[...].astype(F32), axis=0)

    sigma = jax.nn.sigmoid(pre)
    db[a] = (dh_ref[...].astype(F32) * sigma * (1.0 + pre * (1.0 - sigma))).astype(BF16)
    each(lambda o: d_copy(o, a).start(), (2, 6, 1, 3, 5, 7, 4))
    hid_ref[...] = (pre * sigma).astype(BF16)
    each(lambda o: d_copy(o, behind(a, o)).wait_recv())

    d_pre = db[...].reshape(N * OWN, H)
    grad = jnp.dot(x, d_pre, preferred_element_type=F32).reshape(N, ROWS, H)
    grad = jnp.concatenate([grad[:, :, :TILE], grad[:, :, TILE:]], axis=1)
    qf[...] = grad
    qs[...] = grad.astype(BF16)
    each(lambda o: q_copy(o, b).start())
    qr[b] = jnp.zeros((2 * ROWS, TILE), BF16)
    each(lambda o: q_copy(o, behind(b, o)).wait_recv())
    mine = qf[b] + jnp.sum(qr[...].astype(F32), axis=0)

    es[...] = mine.astype(BF16)
    each(lambda o: e_copy(o, rep).start())
    er[rep] = mine.astype(BF16)
    @pl.when(b == rep)
    def _():
        each(lambda o: w_copy(o, b).wait_send())

    each(lambda o: v_copy(o, rep).wait_send())
    each(lambda o: x_copy(o, b).wait_send())
    each(lambda o: p_copy(o, a).wait_send())
    each(lambda o: d_copy(o, a).wait_send())
    each(lambda o: e_copy(o, behind(rep, o)).wait_recv())
    total = jnp.sum(er[...].astype(F32), axis=0)
    total = jnp.concatenate([total[:ROWS], total[ROWS:]], axis=1)
    gs_ref[...] = total[:WIDTH]
    gn_ref[:8] = total[16:]
    gn_ref[8:] = total[WIDTH:16]

    each(lambda o: q_copy(o, b).wait_send())
    each(lambda o: e_copy(o, rep).wait_send())


def write_kernel(hid_in, gs_in, gn_in, hid_out, gs_out, gn_out, hid, gs, gn, sems):
    moves = [(hid_in, hid, hid_out), (gs_in, gs, gs_out), (gn_in, gn, gn_out)]
    reads = [pltpu.make_async_copy(src, mid, sems.at[i]) for i, (src, mid, _) in enumerate(moves)]
    writes = [pltpu.make_async_copy(mid, dst, sems.at[3 + i]) for i, (_, mid, dst) in enumerate(moves)]
    for read in reads:
        read.start()
    for read, write in zip(reads, writes):
        read.wait()
        write.start()
    for write in writes:
        write.wait()


def local(features, w_self, w_neighbor, tile_list, nbr_slot, seed_ids, d_hidden):
    vmem = pl.BlockSpec(memory_space=pltpu.VMEM)
    dma = pltpu.SemaphoreType.DMA
    results = pl.pallas_call(
        sage_kernel,
        out_shape=(
            jax.ShapeDtypeStruct((OWN, H), BF16),
            jax.ShapeDtypeStruct((WIDTH, H), F32),
            jax.ShapeDtypeStruct((WIDTH, H), F32),
        ),
        in_specs=[pl.BlockSpec(memory_space=pltpu.HBM)] * 7,
        out_specs=(vmem,) * 3,
        scratch_shapes=[
            pltpu.VMEM((WIDTH, NS * TILE), BF16),
            pltpu.SMEM((LISTED, TB), jnp.int32),
            pltpu.VMEM((FAN, TB * TILE), jnp.int32),
            pltpu.VMEM((TB, 1, TILE), jnp.int32),
            pltpu.VMEM((WIDTH, H), BF16),
            pltpu.VMEM((WIDTH, H), BF16),
            pltpu.VMEM((OWN, H), BF16),
            pltpu.VMEM((NS, 16, TILE), F32),
            pltpu.VMEM((WIDTH, TILE, NS), BF16),
            pltpu.VMEM((3 * ROWS, TILE), F32),
            pltpu.VMEM((N, BLOCK, TILE), BF16),
            pltpu.VMEM((N, BLOCK, TILE), BF16),
            pltpu.VMEM((N, 2 * ROWS, TILE), BF16),
            pltpu.VMEM((N, OWN, H), F32),
            pltpu.VMEM((N, OWN, H), BF16),
            pltpu.VMEM((N, OWN, H), BF16),
            pltpu.VMEM((N, OWN, H), BF16),
            pltpu.VMEM((N, 2 * ROWS, TILE), F32),
            pltpu.VMEM((N, 2 * ROWS, TILE), BF16),
            pltpu.VMEM((N, 2 * ROWS, TILE), BF16),
            pltpu.VMEM((2 * ROWS, TILE), BF16),
            pltpu.VMEM((N, 2 * ROWS, TILE), BF16),
        ]
        + [dma((CHUNKS + 6,))] + [dma((N,))] * 14,
        compiler_params=pltpu.CompilerParams(
            collective_id=0, has_side_effects=True, vmem_limit_bytes=63 * 2**20
        ),
        name="exchange",
    )(
        features[0], tile_list.T, nbr_slot.T, seed_ids.reshape(TB, 1, TILE), w_self, w_neighbor, d_hidden
    )
    return pl.pallas_call(
        write_kernel,
        out_shape=tuple(jax.ShapeDtypeStruct(r.shape, r.dtype) for r in results),
        in_specs=[pl.BlockSpec(memory_space=pl.ANY)] * 3,
        out_specs=(pl.BlockSpec(memory_space=pl.ANY),) * 3,
        scratch_shapes=[pltpu.VMEM(r.shape, r.dtype) for r in results] + [dma((6,))],
        compiler_params=pltpu.CompilerParams(vmem_limit_bytes=63 * 2**20),
        name="write",
    )(*results)


def solution(mesh):
    placed = (
        P("rep", "feat", None),
        P("feat", None),
        P("feat", None),
        P("rep", None),
        P("rep", None),
        P("rep"),
        P(("rep", "feat"), None),
    )
    return jax.shard_map(
        local,
        mesh=mesh,
        in_specs=placed,
        out_specs=(P(("rep", "feat"), None), P("feat", None), P("feat", None)),
        check_vma=False,
    )
```
